128 devices in a mesh: dp: 16 (over z, y), expert: 8 (over x, core).
Axes of the slice: x: 4, y: 4, z: 4, core: 2. Of those that a mesh axis runs over, the one named last changes fastest.
Arguments:
- tokens: bfloat16 [16384, 2048], P(('dp', 'expert')), may hold values from -6 to 6
- d_out: bfloat16 [16384, 2048], P(('dp', 'expert')), may hold values from -1.25 to 1.25
- expert_ids: int32 [16384, 8], P(('dp', 'expert')), may hold values from 0 to 127, all different within a row; in each aligned block of 128 rows (0 to 127, 128 to 255, ...) at most 9 rows name the same one
- gate_num: int32 [16384, 8], P(('dp', 'expert')), may hold values from 32 to 255
- w_gate: bfloat16 [128, 2048, 768], P(('dp', 'expert')), may hold values from -0.125 to 0.125
- w_up: bfloat16 [128, 2048, 768], P(('dp', 'expert')), may hold values from -0.125 to 0.125
- w_down: bfloat16 [128, 768, 2048], P(('dp', 'expert')), may hold values from -0.21875 to 0.21875
Outputs:
- d_tokens: bfloat16 [16384, 2048], P(('dp', 'expert'))
- d_gate: bfloat16 [16384, 8], P(('dp', 'expert'))
- d_w_gate: bfloat16 [128, 2048, 768], P(('dp', 'expert'))
- d_w_up: bfloat16 [128, 2048, 768], P(('dp', 'expert'))
- d_w_down: bfloat16 [128, 768, 2048], P(('dp', 'expert'))
The draws below stay inside these ranges and needn't reach their ends.
Inputs may be any that keep to these rules, and one draw needn't show every extreme that they name: `expert_ids`: each row names 8 different experts; within the rows of one device no expert is named by more than 9 rows, a bound that some block reaches.
All inputs are finite; a program needn't handle non-finite values.
Results may differ from the reference program's by a relative error of at most 0.0058.
Values may be sent and summed in bfloat16 or wider, within the bound.
No kernel may reach another device: no remote copies, remote signals or barrier semaphores. Data moves between devices by JAX's collectives and lax.ppermute only.
A program may use at most 128 MiB of HBM per device.

```python
import math
import jax
import jax.numpy as jnp
import numpy as np
from jax import lax

D = 2048
F = 768
TOP = 8
TOK_DEV = 128
E = 128
CAP = 9
TOKENS = 16384


def touch_ends(array, rng, low, largest):
    index_at = [jax.random.randint(jax.random.fold_in(rng, axis), (), 0, length) for axis, length in enumerate(array.shape)]
    main_axis = array.shape.index(max(array.shape))
    next_to = index_at[:main_axis] + [(index_at[main_axis] + 1) % array.shape[main_axis]] + index_at[main_axis + 1:]
    return array.at[tuple(index_at)].set(low).at[tuple(next_to)].set(largest)


def levels(rng, dims, shards, least, largest):
    loudness = 1.0
    for axis_at, blocks in shards:
        steps = jax.random.uniform(jax.random.fold_in(jax.random.fold_in(rng, 6), axis_at), (blocks,), jnp.float32, least / len(shards), largest / len(shards))
        loudness = loudness * jnp.repeat(jnp.exp(steps), dims[axis_at] // blocks).reshape((-1,) + (1,) * (len(dims) - 1 - axis_at))
    return loudness


def assign_block(stream_key, own, number, rows, amount, top, reach, slope):
    order = jax.random.permutation(stream_key, amount)
    crowded, usual = portions_of(amount, rows * top, reach, slope, True), portions_of(amount, rows * top, reach, slope, False)
    places = jnp.arange(amount)

    def named(tallies, offset_by):
        used = int((tallies > 0).sum())
        fixed = max(1, used // 4)
        passed = fixed + (places - fixed + offset_by * (used - fixed)) % max(1, amount - fixed)
        return jnp.zeros((amount,), jnp.int32).at[order[jnp.where(places < fixed, places, passed)]].set(jnp.asarray(tallies, jnp.int32))

    tallies = jnp.where(number % 4 == 0, named(crowded, number // 4), named(usual, number - number // 4 - 1))
    mixed = jax.random.permutation(jax.random.fold_in(own, 3), amount)
    donor, receiver = mixed[0:amount // 2 * 2:2], mixed[1:amount // 2 * 2:2]
    room = jnp.minimum(tallies[donor] - 1, reach - tallies[receiver]) // 2
    room = jnp.where((donor == order[0]) | (receiver == order[0]) | (tallies[receiver] == 0), 0, jnp.maximum(room, 0))
    passed = jax.random.randint(jax.random.fold_in(own, 4), (amount // 2,), 0, 1 << 20) % (room + 1)
    tallies = tallies.at[donor].add(-passed).at[receiver].add(passed)
    labels = jnp.searchsorted(jnp.cumsum(tallies), jnp.arange(rows * top), side="right").astype(jnp.int32)
    listing = labels.reshape(top, rows).T
    listing = listing[jax.random.permutation(jax.random.fold_in(own, 1), rows)]
    offset_by = jax.random.randint(jax.random.fold_in(own, 2), (rows, 1), 0, top)
    return jnp.take_along_axis(listing, (jnp.arange(top)[None, :] + offset_by) % top, axis=1)


def portions_of(number_of, total, reach, skew, full):
    loads = [(1 << 20) // math.isqrt(standing ** skew) + 1 for standing in range(1, number_of + 1)]
    largest = reach if full else min(reach, max(-(-total // number_of), total * loads[0] // sum(loads)))
    least = 1 if total - largest >= number_of - 1 else 0
    given, spare = [largest] + [least] * (number_of - 1), total - largest - least * (number_of - 1)
    while spare > 0:
        movable = [i for i in range(1, number_of) if given[i] < largest] or [i for i in range(1, number_of) if given[i] < reach]
        whole, left = sum([loads[i] for i in movable]), spare
        for i in movable:
            more = min(reach - given[i], max(1, left * loads[i] // whole), spare)
            given[i] = given[i] + more
            spare = spare - more
    return np.array(given)


def scatter_about(own_key, shape, scale, bound, cuts=(), kind=jnp.bfloat16):
    values = jax.random.normal(own_key, shape, jnp.float32) * scale
    if len(cuts) > 0:
        values = levels(own_key, shape, cuts, -0.22, 0.18) * values
    return jnp.clip(values, min=-bound, max=bound).astype(kind)


def setup_inputs(seed: int = 0) -> dict:
    key_of = jax.random.split(jax.random.key(seed), 8)
    tokens = scatter_about(key_of[0], (TOKENS, D), 1.0, 6.0, ((0, 128),))
    d_out = scatter_about(key_of[1], (TOKENS, D), 0.2, 1.25, ((0, 128),))
    expert_ids_keys = jax.random.split(jax.random.fold_in(key_of[2], 1), TOKENS // TOK_DEV)
    expert_ids_turns = jax.random.permutation(jax.random.fold_in(key_of[2], 3), TOKENS // TOK_DEV)
    expert_ids = jax.vmap(lambda own, number: assign_block(jax.random.fold_in(key_of[2], 2), own, number, TOK_DEV, E, TOP, CAP, 2))(expert_ids_keys, expert_ids_turns).reshape((TOKENS, TOP))
    gate_num = touch_ends(jax.random.randint(key_of[3], (TOKENS, TOP), 32, 256), jax.random.fold_in(key_of[3], 1), 32, 255).astype(jnp.int32)
    w_gate = scatter_about(key_of[4], (E, D, F), D ** -0.5, 0.125, ((0, 128),))
    w_up = scatter_about(key_of[5], (E, D, F), D ** -0.5, 0.125, ((0, 128),))
    w_down = scatter_about(key_of[6], (E, F, D), F ** -0.5, 0.21875, ((0, 128),))
    return {"tokens": tokens, "d_out": d_out, "expert_ids": expert_ids, "gate_num": gate_num, "w_gate": w_gate, "w_up": w_up, "w_down": w_down}


gate_scale = 1.0 / 256.0


def expert_grads(rows_x, rows_dy, rows_gate, wg, wu, wd):
    contract_rows = (((0,), (0,)), ((), ()))
    contract_cols = (((1,), (1,)), ((), ()))
    pre_gate = jnp.dot(rows_x, wg, preferred_element_type=jnp.float32)
    pre_up = jnp.dot(rows_x, wu, preferred_element_type=jnp.float32)
    sig = jax.nn.sigmoid(pre_gate)
    active = pre_gate * sig
    hidden = active * pre_up
    back = lax.dot_general(rows_dy, wd, contract_cols, preferred_element_type=jnp.float32)
    gate_grad = jnp.sum(back * hidden, axis=1).astype(jnp.bfloat16)
    scaled = rows_gate[:, None] * back
    weighted = (rows_gate[:, None] * hidden).astype(jnp.bfloat16)
    grad_a = (scaled * pre_up * sig * (1.0 + pre_gate * (1.0 - sig))).astype(jnp.bfloat16)
    grad_b = (scaled * active).astype(jnp.bfloat16)
    grad_down = lax.dot_general(weighted, rows_dy, contract_rows, preferred_element_type=jnp.float32).astype(jnp.bfloat16)
    grad_gate = lax.dot_general(rows_x, grad_a, contract_rows, preferred_element_type=jnp.float32).astype(jnp.bfloat16)
    grad_up = lax.dot_general(rows_x, grad_b, contract_rows, preferred_element_type=jnp.float32).astype(jnp.bfloat16)
    row_grad = lax.dot_general(grad_a, wg, contract_cols, preferred_element_type=jnp.float32)
    row_grad = (row_grad + lax.dot_general(grad_b, wu, contract_cols, preferred_element_type=jnp.float32)).astype(jnp.bfloat16)
    return row_grad, gate_grad, grad_gate, grad_up, grad_down


def reference(tokens, d_out, expert_ids, gate_num, w_gate, w_up, w_down):
    blocks = TOKENS // TOK_DEV
    routes = TOK_DEV * TOP
    ids = expert_ids.reshape(blocks, routes).astype(jnp.int32)
    onehot = (ids[:, :, None] == jnp.arange(E, dtype=jnp.int32)[None, None, :]).astype(jnp.int32)
    position = jnp.sum(jnp.cumsum(onehot, axis=1) * onehot, axis=2) - 1
    column = jnp.arange(blocks, dtype=jnp.int32)[:, None] * CAP + position
    owner = jnp.full((E, blocks * CAP), -1, jnp.int32)
    owner = owner.at[ids.reshape(-1), column.reshape(-1)].set(jnp.arange(TOKENS * TOP, dtype=jnp.int32))
    gate = gate_num.reshape(-1).astype(jnp.float32) * gate_scale

    def per_expert(carry, inputs):
        grad_rows, grad_gates = carry
        owner_row, wg, wu, wd = inputs
        valid = owner_row >= 0
        safe = jnp.where(valid, owner_row, 0).astype(jnp.int32)
        row = (safe // TOP).astype(jnp.int32)
        rows_x = jnp.where(valid[:, None], tokens[row], jnp.zeros((), tokens.dtype))
        rows_dy = jnp.where(valid[:, None], d_out[row], jnp.zeros((), d_out.dtype))
        rows_gate = jnp.where(valid, gate[safe], 0.0)
        row_grad, gate_grad, grad_gate, grad_up, grad_down = expert_grads(rows_x, rows_dy, rows_gate, wg, wu, wd)
        grad_rows = grad_rows.at[row].add(jnp.where(valid[:, None], row_grad.astype(jnp.float32), 0.0))
        target = jnp.where(valid, owner_row, TOKENS * TOP).astype(jnp.int32)
        grad_gates = grad_gates.at[target].add(jnp.where(valid, gate_grad.astype(jnp.float32), 0.0))
        return (grad_rows, grad_gates), (grad_gate, grad_up, grad_down)

    start = (jnp.zeros((TOKENS, D), jnp.float32), jnp.zeros((TOKENS * TOP + 1,), jnp.float32))
    (grad_rows, grad_gates), (d_w_gate, d_w_up, d_w_down) = lax.scan(per_expert, start, (owner, w_gate, w_up, w_down))
    d_tokens = grad_rows.astype(jnp.bfloat16)
    d_gate = grad_gates[:TOKENS * TOP].reshape(TOKENS, TOP).astype(jnp.bfloat16)
    return d_tokens, d_gate, d_w_gate, d_w_up, d_w_down
```

```python
import functools

import jax
import jax.numpy as jnp
from jax import lax
from jax.experimental import pallas as pl
from jax.experimental.pallas import tpu as pltpu
from jax.sharding import PartitionSpec as P

bf16 = jnp.bfloat16
f32 = jnp.float32
lanes = 128
sub = 16
capacity = 9
first_rows = 7
contract_rows = (((0,), (0,)), ((), ()))
contract_cols = (((1,), (1,)), ((), ()))


def params(mib):
    return pltpu.CompilerParams(vmem_limit_bytes=mib * 1024 * 1024)


def whole(shape):
    return pl.BlockSpec(shape, lambda *_: (0,) * len(shape))


def swap_matrix():
    size = sub * sub
    row = lax.broadcasted_iota(jnp.int32, (size, size), 0)
    col = lax.broadcasted_iota(jnp.int32, (size, size), 1)
    return jnp.where(((row & 15) << 4) + (row >> 4) == col, 1.0, 0.0).astype(bf16)


def spread_tables(ids, num, experts):
    top, toks = ids.shape
    gate = num.astype(f32) * (1.0 / 256.0)
    expert_at = lax.broadcasted_iota(jnp.int32, (experts, toks), 0)
    named = jnp.zeros((experts, toks), f32)
    gates = jnp.zeros((experts, toks), f32)
    for k in range(top):
        hit = ids[k : k + 1, :] == expert_at
        named = jnp.where(hit, 1.0, named)
        gates = jnp.where(hit, gate[k : k + 1, :], gates)
    row = lax.broadcasted_iota(jnp.int32, (toks, toks), 0)
    col = lax.broadcasted_iota(jnp.int32, (toks, toks), 1)
    before = jnp.where(row < col, 1.0, 0.0).astype(bf16)
    place = jnp.dot(named.astype(bf16), before, preferred_element_type=f32)
    token = lax.broadcasted_iota(jnp.int32, (experts, toks), 1).astype(f32)
    here = [(named > 0.0) & (place == float(p)) for p in range(capacity)]
    wanted = lax.broadcasted_iota(jnp.int32, (sub, capacity * toks), 0)
    owner = lax.broadcasted_iota(jnp.int32, (sub, capacity * toks), 1) >> 7
    collect = jnp.where(owner == wanted, 1.0, 0.0).astype(bf16)
    index, scale = [
        lax.dot_general(
            collect,
            jnp.concatenate([jnp.where(h, v, 0.0).astype(bf16) for h in here], axis=1),
            contract_cols,
            preferred_element_type=f32,
        )
        for v in (token, gates)
    ]
    code = (expert_at * sub).astype(f32) + place
    codes = [
        jnp.sum(jnp.where(ids[k : k + 1, :] == expert_at, code, 0.0), axis=0, keepdims=True)
        for k in range(top)
    ]
    return index.astype(jnp.int32), scale, jnp.concatenate(codes, axis=0).astype(jnp.int32)


def wide_to_tiles(swap, wide, chunks, store):
    rows = wide.shape[0]
    for r in range(0, rows, 2 * sub):
        halves = [
            jnp.concatenate(
                [wide[r + d : r + d + sub, j * lanes : (j + 1) * lanes] for j in range(chunks)], axis=0
            )
            for d in (0, sub)
        ]
        tiles = jnp.dot(swap, jnp.concatenate(halves, axis=1), preferred_element_type=f32)
        store(r, tiles[:, :lanes].reshape(sub, chunks, lanes))
        store(r + sub, tiles[:, lanes:].reshape(sub, chunks, lanes))


def make_tiles(tok_ref, dy_ref, tok_tiles, dy_tiles):
    swap = swap_matrix()
    chunks = tok_ref.shape[1] // lanes

    def put_tok(r, tiles):
        tok_tiles[r : r + sub] = tiles.astype(bf16)

    def put_dy(r, tiles):
        dy_tiles[r : r + sub] = tiles

    wide_to_tiles(swap, tok_ref, chunks, put_tok)
    wide_to_tiles(swap, dy_ref, chunks, put_dy)


def fill_rows(start, count, index_ref, scale_ref, tok_tiles, dy_tiles, out_ref):
    group = out_ref.shape[0]
    first = pl.program_id(0) * group

    def one(e, carry):
        for p in range(count):
            token = index_ref[start + p, first + e]
            scale = scale_ref[start + p, first + e]
            out_ref[e, p * sub : (p + 1) * sub, :] = tok_tiles[token]
            at = (count + p) * sub
            out_ref[e, at : at + sub, :] = (dy_tiles[token] * scale).astype(bf16)
        return carry

    lax.fori_loop(0, group, one, 0)


def pack_first_kernel(
    start, count, ids_ref, num_ref, tok_ref, dy_ref,
    out_ref, index_ref, scale_ref, code_ref, tok_tiles, dy_tiles, index_s, scale_s, sems,
):
    @pl.when(pl.program_id(0) == 0)
    def _():
        index, scale, code = spread_tables(ids_ref[...], num_ref[...], index_ref.shape[1])
        index_ref[...] = index
        scale_ref[...] = scale
        code_ref[...] = code
        one = pltpu.make_async_copy(index_ref, index_s, sems.at[0])
        two = pltpu.make_async_copy(scale_ref, scale_s, sems.at[1])
        one.start()
        two.start()
        make_tiles(tok_ref, dy_ref, tok_tiles, dy_tiles)
        one.wait()
        two.wait()

    fill_rows(start, count, index_s, scale_s, tok_tiles, dy_tiles, out_ref)


def pack_rest_kernel(
    start, count, index_ref, scale_ref, tok_ref, dy_ref, out_ref, tok_tiles, dy_tiles
):
    @pl.when(pl.program_id(0) == 0)
    def _():
        make_tiles(tok_ref, dy_ref, tok_tiles, dy_tiles)

    fill_rows(start, count, index_ref, scale_ref, tok_tiles, dy_tiles, out_ref)


def pack(tokens, d_out, start, count, experts, ids=None, num=None, tables=None):
    toks, width = tokens.shape
    chunks = width // lanes
    group = 16
    out_shape = [jax.ShapeDtypeStruct((experts, 2 * count * sub, lanes), bf16)]
    out_specs = [pl.BlockSpec((group, 2 * count * sub, lanes), lambda i: (i, 0, 0))]
    scratch = [
        pltpu.VMEM((toks, chunks, lanes), bf16),
        pltpu.VMEM((toks, chunks, lanes), f32),
    ]
    if tables is None:
        body = functools.partial(pack_first_kernel, start, count)
        args = (ids, num, tokens, d_out)
        in_specs = [whole(a.shape) for a in args]
        out_shape += [
            jax.ShapeDtypeStruct((sub, experts), jnp.int32),
            jax.ShapeDtypeStruct((sub, experts), f32),
            jax.ShapeDtypeStruct(ids.shape, jnp.int32),
        ]
        out_specs += [whole(o.shape) for o in out_shape[1:]]
        scratch += [
            pltpu.SMEM((sub, experts), jnp.int32),
            pltpu.SMEM((sub, experts), f32),
            pltpu.SemaphoreType.DMA((2,)),
        ]
    else:
        body = functools.partial(pack_rest_kernel, start, count)
        args = (*tables, tokens, d_out)
        in_specs = [pl.BlockSpec(memory_space=pltpu.SMEM)] * 2 + [whole(tokens.shape)] * 2
    return pl.pallas_call(
        body,
        grid=(experts // group,),
        in_specs=in_specs,
        out_specs=out_specs,
        out_shape=out_shape,
        scratch_shapes=scratch,
        compiler_params=params(60),
        cost_estimate=pl.CostEstimate(
            flops=0, bytes_accessed=4 * experts * count * width, transcendentals=0
        ),
        name="pack_first" if tables is None else "pack_rest",
    )(*args)


def expert_kernel(start, count, block, last, *refs):
    (wire_hbm, wg_hbm, wu_hbm, wd_hbm) = refs[:4]
    refs = refs[4:]
    if last:
        old_gate_ref = refs[0]
        refs = refs[7:]
    out_hbm = refs[:5]
    back_ref = refs[5]
    refs = refs[6:]
    if not last:
        gate_ref = refs[0]
        refs = refs[1:]
    (wire, wg, wu, wd, x_ref, dy_ref, h_ref, da_ref, db_ref, dx_ref, swap_ref) = refs[:11]
    (wire_sem, weight_sem, out_sem) = refs[11:]
    sources = wire_hbm.shape[0]
    blocks = sources // block
    rows = block * count
    width, hidden = wg.shape
    chunks = width // lanes
    part = 256
    half = count * sub

    def wire_copy(b, side):
        at = (slice(b * block, (b + 1) * block), slice(side * half, (side + 1) * half))
        return pltpu.make_async_copy(wire_hbm.at[at], wire.at[at], wire_sem.at[b, side])

    weights = [
        pltpu.make_async_copy(src, dst, weight_sem.at[i])
        for i, (src, dst) in enumerate(((wg_hbm, wg), (wu_hbm, wu), (wd_hbm, wd)))
    ]

    def out_copy(i, b):
        src = (x_ref, dy_ref, h_ref, da_ref, db_ref)[i]
        to = sources * start + b * rows
        return pltpu.make_async_copy(
            src.at[b * rows : (b + 1) * rows], out_hbm[i].at[to : to + rows], out_sem.at[i, b]
        )

    wire_copy(0, 0).start()
    weights[0].start()
    weights[1].start()
    wire_copy(0, 1).start()
    weights[2].start()
    for b in range(1, blocks):
        wire_copy(b, 0).start()
        wire_copy(b, 1).start()
    swap_ref[...] = swap_matrix()

    def widen(b, side, out):
        def step(p, carry):
            at = pl.multiple_of(side * half + p * sub, sub)
            for s in range(0, block, 2 * sub):
                tiles = jnp.concatenate(
                    [
                        wire[b * block + s + d : b * block + s + d + sub, pl.ds(at, sub), :].reshape(
                            sub * sub, lanes
                        )
                        for d in (0, sub)
                    ],
                    axis=1,
                )
                flat = jnp.dot(swap_ref[...], tiles, preferred_element_type=f32).astype(bf16)
                for d in (0, 1):
                    to = pl.multiple_of(b * rows + p * block + s + d * sub, sub)
                    for j in range(chunks):
                        out[pl.ds(to, sub), j * lanes : (j + 1) * lanes] = flat[
                            j * sub : (j + 1) * sub, d * lanes : (d + 1) * lanes
                        ]
            return carry

        lax.fori_loop(0, count, step, 0)

    for b in range(blocks):
        low, high = b * rows, (b + 1) * rows
        wire_copy(b, 0).wait()
        widen(b, 0, x_ref)
        out_copy(0, b).start()
        wire_copy(b, 1).wait()
        widen(b, 1, dy_ref)
        out_copy(1, b).start()
        if b == 0:
            for copy in weights:
                copy.wait()

        gate_grad = jnp.zeros((rows, 1), f32)
        for n in range(0, hidden, part):
            x = x_ref[low:high]
            a = jnp.dot(x, wg[:, n : n + part], preferred_element_type=f32)
            up = jnp.dot(x, wu[:, n : n + part], preferred_element_type=f32)
            u = lax.dot_general(
                dy_ref[low:high], wd[n : n + part, :], contract_cols, preferred_element_type=f32
            )
            sig = jax.nn.sigmoid(a)
            active = a * sig
            h = active * up
            gate_grad = gate_grad + jnp.sum(u * h, axis=1, keepdims=True)
            h_ref[low:high, n : n + part] = h.astype(bf16)
            da_ref[low:high, n : n + part] = (u * up * sig * (1.0 + a * (1.0 - sig))).astype(bf16)
            db_ref[low:high, n : n + part] = (u * active).astype(bf16)
        for i in (2, 3, 4):
            out_copy(i, b).start()

        lane = lax.broadcasted_iota(jnp.int32, (block, lanes), 1)
        at = slice(b * block, (b + 1) * block)
        gates = old_gate_ref[at, :] if last else jnp.zeros((block, lanes), f32)
        for p in range(count):
            gates = jnp.where(lane == start + p, gate_grad[p * block : (p + 1) * block], gates)
        if last:
            eight = jnp.broadcast_to(gates[:, None, :], (block, 8, lanes))
            back_ref[at, half : half + 8, :] = eight.astype(bf16)
        else:
            gate_ref[at, :] = gates

        for n in range(0, width, part):
            dx = lax.dot_general(
                da_ref[low:high], wg[n : n + part, :], contract_cols, preferred_element_type=f32
            )
            dx = dx + lax.dot_general(
                db_ref[low:high], wu[n : n + part, :], contract_cols, preferred_element_type=f32
            )
            dx_ref[:, n : n + part] = dx.astype(bf16)

        def narrow(p, carry):
            to = pl.multiple_of(p * sub, sub)
            for s in range(0, block, 2 * sub):
                halves = []
                for d in (0, sub):
                    row = pl.multiple_of(p * block + s + d, sub)
                    halves.append(
                        jnp.concatenate(
                            [
                                dx_ref[pl.ds(row, sub), j * lanes : (j + 1) * lanes]
                                for j in range(chunks)
                            ],
                            axis=0,
                        )
                    )
                tiles = jnp.dot(
                    swap_ref[...], jnp.concatenate(halves, axis=1), preferred_element_type=f32
                ).astype(bf16)
                for d in (0, 1):
                    e = b * block + s + d * sub
                    back_ref[e : e + sub, pl.ds(to, sub), :] = tiles[
                        :, d * lanes : (d + 1) * lanes
                    ].reshape(sub, sub, lanes)
            return carry

        lax.fori_loop(0, count, narrow, 0)

    for b in range(blocks):
        for i in range(5):
            out_copy(i, b).wait()


def expert_rows(wire, wg, wu, wd, start, count, block, carry=None):
    sources = wire.shape[0]
    width, hidden = wg.shape
    mine = sources * count
    last = carry is not None
    total = sources * capacity
    anywhere = pl.BlockSpec(memory_space=pl.ANY)
    high = count * sub + (8 if last else 0)
    back_spec = pl.BlockSpec(
        (pl.Element(sources), pl.Element(high), pl.Element(lanes)),
        lambda i: (0, start * sub, 0),
    )
    out_shape = [
        jax.ShapeDtypeStruct((total, width), bf16),
        jax.ShapeDtypeStruct((total, width), bf16),
        jax.ShapeDtypeStruct((total, hidden), bf16),
        jax.ShapeDtypeStruct((total, hidden), bf16),
        jax.ShapeDtypeStruct((total, hidden), bf16),
        jax.ShapeDtypeStruct((sources, capacity * sub + 8, lanes), bf16),
    ]
    out_specs = [anywhere] * 5 + [back_spec]
    in_specs = [anywhere] * 4
    args = [wire, wg, wu, wd]
    aliases = {}
    if last:
        in_specs += [whole((sources, lanes))] + [anywhere] * 6
        args += [carry[6]] + list(carry[:6])
        aliases = {5 + i: i for i in range(6)}
    else:
        out_specs.append(whole((sources, lanes)))
        out_shape.append(jax.ShapeDtypeStruct((sources, lanes), f32))
    return pl.pallas_call(
        functools.partial(expert_kernel, start, count, block, last),
        grid=(1,),
        in_specs=in_specs,
        out_specs=out_specs,
        out_shape=out_shape,
        scratch_shapes=[
            pltpu.VMEM(wire.shape, bf16),
            pltpu.VMEM((width, hidden), bf16),
            pltpu.VMEM((width, hidden), bf16),
            pltpu.VMEM((hidden, width), bf16),
            pltpu.VMEM((mine, width), bf16),
            pltpu.VMEM((mine, width), bf16),
            pltpu.VMEM((mine, hidden), bf16),
            pltpu.VMEM((mine, hidden), bf16),
            pltpu.VMEM((mine, hidden), bf16),
            pltpu.VMEM((block * count, width), bf16),
            pltpu.VMEM((sub * sub, sub * sub), bf16),
            pltpu.SemaphoreType.DMA((sources // block, 2)),
            pltpu.SemaphoreType.DMA((3,)),
            pltpu.SemaphoreType.DMA((5, sources // block)),
        ],
        input_output_aliases=aliases,
        compiler_params=params(60),
        cost_estimate=pl.CostEstimate(
            flops=10 * mine * width * hidden,
            bytes_accessed=6 * width * hidden + 12 * mine * width,
            transcendentals=mine * hidden,
        ),
        name="expert_rows_last" if last else "expert_rows_first",
    )(*args)


def combine_kernel(code_s_ref, code_ref, num_ref, back_ref, tok_ref, gate_ref, tiles_ref):
    toks, width = tok_ref.shape
    top = code_ref.shape[0]
    chunks = width // lanes
    experts = back_ref.shape[0]

    def one(t, carry):
        total = None
        for k in range(top):
            code = code_s_ref[k, t]
            at = pl.multiple_of((code & 15) << 4, sub)
            row = back_ref[code >> 4, pl.ds(at, sub), :].astype(f32)
            total = row if total is None else total + row
        tiles_ref[t] = total.astype(bf16)
        return carry

    lax.fori_loop(0, toks, one, 0, unroll=4)
    swap = swap_matrix()
    for r in range(0, toks, 2 * sub):
        tiles = jnp.concatenate(
            [tiles_ref[r + d : r + d + sub].reshape(sub * sub, lanes) for d in (0, sub)], axis=1
        )
        flat = jnp.dot(swap, tiles, preferred_element_type=f32).astype(bf16)
        for d in (0, 1):
            for j in range(chunks):
                tok_ref[r + d * sub : r + (d + 1) * sub, j * lanes : (j + 1) * lanes] = flat[
                    j * sub : (j + 1) * sub, d * lanes : (d + 1) * lanes
                ]

    grads = jnp.max(back_ref[:, capacity * sub : capacity * sub + 8, :].astype(f32), axis=1)
    grads = jnp.transpose(grads).astype(bf16)
    gate = num_ref[...].astype(f32) * (1.0 / 256.0)
    expert_at = lax.broadcasted_iota(jnp.int32, (experts, toks), 0)
    place_at = lax.broadcasted_iota(jnp.int32, (lanes, toks), 0)
    found = []
    for k in range(top):
        code = code_ref[k : k + 1, :]
        hit = jnp.where((code >> 4) == expert_at, 1.0, 0.0).astype(bf16)
        rows = jnp.dot(grads, hit, preferred_element_type=f32)
        found.append(jnp.sum(jnp.where((code & 15) == place_at, rows, 0.0), axis=0, keepdims=True))
    gate_ref[...] = (jnp.concatenate(found, axis=0) / gate).astype(bf16)


def combine(code, num, back, toks, width):
    top = code.shape[0]
    vmem = pl.BlockSpec(memory_space=pltpu.VMEM)
    return pl.pallas_call(
        combine_kernel,
        in_specs=[pl.BlockSpec(memory_space=pltpu.SMEM), vmem, vmem, vmem],
        out_specs=[vmem] * 2,
        out_shape=[
            jax.ShapeDtypeStruct((toks, width), bf16),
            jax.ShapeDtypeStruct((top, toks), bf16),
        ],
        scratch_shapes=[pltpu.VMEM((toks, width // lanes, lanes), bf16)],
        compiler_params=params(60),
        name="combine_rows",
    )(code, code, num, back)


def exchange(rows):
    return lax.all_to_all(rows, ("dp", "expert"), split_axis=0, concat_axis=0, tiled=True)


def local(tokens, d_out, expert_ids, gate_num, w_gate, w_up, w_down):
    toks, width = tokens.shape
    experts = lax.axis_size("dp") * lax.axis_size("expert")
    wg, wu, wd = w_gate[0], w_up[0], w_down[0]
    ids, num = expert_ids.T, gate_num.T
    rest = capacity - first_rows
    first, index, scale, code = pack(tokens, d_out, 0, first_rows, experts, ids, num)
    (second,) = pack(tokens, d_out, first_rows, rest, experts, tables=(index, scale))
    first, second = exchange(first), exchange(second)
    part = expert_rows(first, wg, wu, wd, 0, first_rows, 64)
    rows_x, rows_dy, h, da, db, back = expert_rows(second, wg, wu, wd, first_rows, rest, 128, part)
    back = exchange(back)
    grad_gate = lax.dot_general(rows_x, da, contract_rows, preferred_element_type=f32).astype(bf16)
    grad_up = lax.dot_general(rows_x, db, contract_rows, preferred_element_type=f32).astype(bf16)
    grad_down = lax.dot_general(h, rows_dy, contract_rows, preferred_element_type=f32).astype(bf16)
    d_tokens, d_gate = combine(code, num, back, toks, width)
    return (d_tokens, d_gate.T, grad_gate[None], grad_up[None], grad_down[None])


def solution(mesh):
    rows = P(("dp", "expert"), None)
    blocks = P(("dp", "expert"), None, None)
    return jax.shard_map(
        local,
        mesh=mesh,
        in_specs=(rows, rows, rows, rows, blocks, blocks, blocks),
        out_specs=(rows, rows, blocks, blocks, blocks),
        check_vma=False,
    )
```

```python
import functools

import jax
import jax.numpy as jnp
from jax import lax
from jax.experimental import pallas as pl
from jax.experimental.pallas import tpu as pltpu
from jax.sharding import PartitionSpec as P

bf16 = jnp.bfloat16
f32 = jnp.float32
lanes = 128
sub = 16
capacity = 9
first_rows = 7
contract_rows = (((0,), (0,)), ((), ()))
contract_cols = (((1,), (1,)), ((), ()))


def params(mib):
    return pltpu.CompilerParams(vmem_limit_bytes=mib * 1024 * 1024)


def whole(shape):
    return pl.BlockSpec(shape, lambda *_: (0,) * len(shape))


def swap_matrix():
    size = sub * sub
    row = lax.broadcasted_iota(jnp.int32, (size, size), 0)
    col = lax.broadcasted_iota(jnp.int32, (size, size), 1)
    return jnp.where(((row & 15) << 4) + (row >> 4) == col, 1.0, 0.0).astype(bf16)


def spread_tables(ids, num, experts):
    top, toks = ids.shape
    gate = num.astype(f32) * (1.0 / 256.0)
    expert_at = lax.broadcasted_iota(jnp.int32, (experts, toks), 0)
    named = jnp.zeros((experts, toks), f32)
    gates = jnp.zeros((experts, toks), f32)
    for k in range(top):
        hit = ids[k : k + 1, :] == expert_at
        named = jnp.where(hit, 1.0, named)
        gates = jnp.where(hit, gate[k : k + 1, :], gates)
    row = lax.broadcasted_iota(jnp.int32, (toks, toks), 0)
    col = lax.broadcasted_iota(jnp.int32, (toks, toks), 1)
    before = jnp.where(row < col, 1.0, 0.0).astype(bf16)
    place = jnp.dot(named.astype(bf16), before, preferred_element_type=f32)
    token = lax.broadcasted_iota(jnp.int32, (experts, toks), 1).astype(f32)
    here = [(named > 0.0) & (place == float(p)) for p in range(capacity)]
    wanted = lax.broadcasted_iota(jnp.int32, (sub, capacity * toks), 0)
    owner = lax.broadcasted_iota(jnp.int32, (sub, capacity * toks), 1) >> 7
    collect = jnp.where(owner == wanted, 1.0, 0.0).astype(bf16)
    index, scale = [
        lax.dot_general(
            collect,
            jnp.concatenate([jnp.where(h, v, 0.0).astype(bf16) for h in here], axis=1),
            contract_cols,
            preferred_element_type=f32,
        )
        for v in (token, gates)
    ]
    code = (expert_at * sub).astype(f32) + place
    codes = [
        jnp.sum(jnp.where(ids[k : k + 1, :] == expert_at, code, 0.0), axis=0, keepdims=True)
        for k in range(top)
    ]
    return index.astype(jnp.int32), scale, jnp.concatenate(codes, axis=0).astype(jnp.int32)


def wide_to_tiles(swap, wide, chunks, store):
    rows = wide.shape[0]
    for r in range(0, rows, 2 * sub):
        halves = [
            jnp.concatenate(
                [wide[r + d : r + d + sub, j * lanes : (j + 1) * lanes] for j in range(chunks)], axis=0
            )
            for d in (0, sub)
        ]
        tiles = jnp.dot(swap, jnp.concatenate(halves, axis=1), preferred_element_type=f32)
        store(r, tiles[:, :lanes].reshape(sub, chunks, lanes))
        store(r + sub, tiles[:, lanes:].reshape(sub, chunks, lanes))


def make_tiles(tok_ref, dy_ref, tok_tiles, dy_tiles):
    swap = swap_matrix()
    chunks = tok_ref.shape[1] // lanes

    def put_tok(r, tiles):
        tok_tiles[r : r + sub] = tiles.astype(bf16)

    def put_dy(r, tiles):
        dy_tiles[r : r + sub] = tiles

    wide_to_tiles(swap, tok_ref, chunks, put_tok)
    wide_to_tiles(swap, dy_ref, chunks, put_dy)


def fill_rows(start, count, index_ref, scale_ref, tok_tiles, dy_tiles, buffer, out_hbm, sems):
    experts = buffer.shape[0]
    groups = sems.shape[0]
    group = experts // groups

    def out_copy(g):
        at = slice(g * group, (g + 1) * group)
        return pltpu.make_async_copy(buffer.at[at], out_hbm.at[at], sems.at[g])

    def one(e, carry):
        for p in range(count):
            token = index_ref[start + p, e]
            scale = scale_ref[start + p, e]
            buffer[e, p * sub : (p + 1) * sub, :] = tok_tiles[token]
            at = (count + p) * sub
            buffer[e, at : at + sub, :] = (dy_tiles[token] * scale).astype(bf16)
        return carry

    for g in range(groups):
        lax.fori_loop(g * group, (g + 1) * group, one, 0, unroll=2)
        out_copy(g).start()
    for g in range(groups):
        out_copy(g).wait()


def pack_first_kernel(
    start, count, ids_ref, num_ref, tok_ref, dy_ref,
    out_hbm, index_ref, scale_ref, code_ref,
    tok_tiles, dy_tiles, buffer, out_sems, index_s, scale_s, sems,
):
    index, scale, code = spread_tables(ids_ref[...], num_ref[...], index_ref.shape[1])
    index_ref[...] = index
    scale_ref[...] = scale
    code_ref[...] = code
    one = pltpu.make_async_copy(index_ref, index_s, sems.at[0])
    two = pltpu.make_async_copy(scale_ref, scale_s, sems.at[1])
    one.start()
    two.start()
    make_tiles(tok_ref, dy_ref, tok_tiles, dy_tiles)
    one.wait()
    two.wait()
    fill_rows(start, count, index_s, scale_s, tok_tiles, dy_tiles, buffer, out_hbm, out_sems)


def pack_rest_kernel(
    start, count, index_ref, scale_ref, tok_ref, dy_ref,
    out_hbm, tok_tiles, dy_tiles, buffer, out_sems,
):
    make_tiles(tok_ref, dy_ref, tok_tiles, dy_tiles)
    fill_rows(start, count, index_ref, scale_ref, tok_tiles, dy_tiles, buffer, out_hbm, out_sems)


def pack(tokens, d_out, start, count, experts, ids=None, num=None, tables=None):
    toks, width = tokens.shape
    chunks = width // lanes
    wire = (experts, 2 * count * sub, lanes)
    out_shape = [jax.ShapeDtypeStruct(wire, bf16)]
    out_specs = [pl.BlockSpec(memory_space=pl.ANY)]
    scratch = [
        pltpu.VMEM((toks, chunks, lanes), bf16),
        pltpu.VMEM((toks, chunks, lanes), f32),
        pltpu.VMEM(wire, bf16),
        pltpu.SemaphoreType.DMA((8,)),
    ]
    vmem = pl.BlockSpec(memory_space=pltpu.VMEM)
    if tables is None:
        body = functools.partial(pack_first_kernel, start, count)
        args = (ids, num, tokens, d_out)
        in_specs = [vmem] * 4
        out_shape += [
            jax.ShapeDtypeStruct((sub, experts), jnp.int32),
            jax.ShapeDtypeStruct((sub, experts), f32),
            jax.ShapeDtypeStruct(ids.shape, jnp.int32),
        ]
        out_specs += [vmem] * 3
        scratch += [
            pltpu.SMEM((sub, experts), jnp.int32),
            pltpu.SMEM((sub, experts), f32),
            pltpu.SemaphoreType.DMA((2,)),
        ]
    else:
        body = functools.partial(pack_rest_kernel, start, count)
        args = (*tables, tokens, d_out)
        in_specs = [pl.BlockSpec(memory_space=pltpu.SMEM)] * 2 + [vmem] * 2
    return pl.pallas_call(
        body,
        in_specs=in_specs,
        out_specs=out_specs,
        out_shape=out_shape,
        scratch_shapes=scratch,
        compiler_params=params(60),
        cost_estimate=pl.CostEstimate(
            flops=0, bytes_accessed=4 * experts * count * width, transcendentals=0
        ),
        name="pack_first" if tables is None else "pack_rest",
    )(*args)


def expert_kernel(start, count, block, last, *refs):
    (wire_hbm, wg, wu_hbm, wd_hbm) = refs[:4]
    refs = refs[4:]
    if last:
        old_gate_ref = refs[0]
        refs = refs[7:]
    out_hbm = refs[:5]
    back_ref = refs[5]
    refs = refs[6:]
    if not last:
        gate_ref = refs[0]
        refs = refs[1:]
    (wire, wu, wd, x_ref, dy_ref, h_ref, da_ref, db_ref, dx_ref, swap_ref) = refs[:10]
    (wire_sem, weight_sem, out_sem) = refs[10:]
    sources = wire_hbm.shape[0]
    blocks = sources // block
    rows = block * count
    width, hidden = wg.shape
    chunks = width // lanes
    part = 256
    half = count * sub

    def wire_copy(b, side):
        at = (slice(b * block, (b + 1) * block), slice(side * half, (side + 1) * half))
        return pltpu.make_async_copy(wire_hbm.at[at], wire.at[at], wire_sem.at[b, side])

    weights = [
        pltpu.make_async_copy(src, dst, weight_sem.at[i])
        for i, (src, dst) in enumerate(((wu_hbm, wu), (wd_hbm, wd)))
    ]

    def out_copy(i, b):
        src = (x_ref, dy_ref, h_ref, da_ref, db_ref)[i]
        to = sources * start + b * rows
        return pltpu.make_async_copy(
            src.at[b * rows : (b + 1) * rows], out_hbm[i].at[to : to + rows], out_sem.at[i, b]
        )

    wire_copy(0, 0).start()
    weights[0].start()
    wire_copy(0, 1).start()
    weights[1].start()
    for b in range(1, blocks):
        wire_copy(b, 0).start()
        wire_copy(b, 1).start()
    swap_ref[...] = swap_matrix()

    def widen(b, side, out):
        def step(p, carry):
            at = pl.multiple_of(side * half + p * sub, sub)
            for s in range(0, block, 2 * sub):
                tiles = jnp.concatenate(
                    [
                        wire[b * block + s + d : b * block + s + d + sub, pl.ds(at, sub), :].reshape(
                            sub * sub, lanes
                        )
                        for d in (0, sub)
                    ],
                    axis=1,
                )
                flat = jnp.dot(swap_ref[...], tiles, preferred_element_type=f32).astype(bf16)
                for d in (0, 1):
                    to = pl.multiple_of(b * rows + p * block + s + d * sub, sub)
                    for j in range(chunks):
                        out[pl.ds(to, sub), j * lanes : (j + 1) * lanes] = flat[
                            j * sub : (j + 1) * sub, d * lanes : (d + 1) * lanes
                        ]
            return carry

        lax.fori_loop(0, count, step, 0, unroll=True)

    for b in range(blocks):
        low, high = b * rows, (b + 1) * rows
        wire_copy(b, 0).wait()
        widen(b, 0, x_ref)
        out_copy(0, b).start()
        gates_in = [
            jnp.dot(x_ref[low:high], wg[:, n : n + part], preferred_element_type=f32)
            for n in range(0, hidden, part)
        ]
        wire_copy(b, 1).wait()
        widen(b, 1, dy_ref)
        out_copy(1, b).start()
        if b == 0:
            for copy in weights:
                copy.wait()

        gate_grad = jnp.zeros((rows, 1), f32)
        for n in range(0, hidden, part):
            x = x_ref[low:high]
            a = gates_in[n // part]
            up = jnp.dot(x, wu[:, n : n + part], preferred_element_type=f32)
            u = lax.dot_general(
                dy_ref[low:high], wd[n : n + part, :], contract_cols, preferred_element_type=f32
            )
            sig = jax.nn.sigmoid(a)
            active = a * sig
            h = active * up
            gate_grad = gate_grad + jnp.sum(u * h, axis=1, keepdims=True)
            h_ref[low:high, n : n + part] = h.astype(bf16)
            da_ref[low:high, n : n + part] = (u * up * sig * (1.0 + a * (1.0 - sig))).astype(bf16)
            db_ref[low:high, n : n + part] = (u * active).astype(bf16)
        for i in (2, 3, 4):
            out_copy(i, b).start()

        lane = lax.broadcasted_iota(jnp.int32, (block, lanes), 1)
        at = slice(b * block, (b + 1) * block)
        gates = old_gate_ref[at, :] if last else jnp.zeros((block, lanes), f32)
        for p in range(count):
            gates = jnp.where(lane == start + p, gate_grad[p * block : (p + 1) * block], gates)
        if last:
            eight = jnp.broadcast_to(gates[:, None, :], (block, 8, lanes))
            back_ref[at, half : half + 8, :] = eight.astype(bf16)
        else:
            gate_ref[at, :] = gates

        for n in range(0, width, part):
            dx = lax.dot_general(
                da_ref[low:high], wg[n : n + part, :], contract_cols, preferred_element_type=f32
            )
            dx = dx + lax.dot_general(
                db_ref[low:high], wu[n : n + part, :], contract_cols, preferred_element_type=f32
            )
            dx_ref[:, n : n + part] = dx.astype(bf16)

        def narrow(p, carry):
            to = pl.multiple_of(p * sub, sub)
            for s in range(0, block, 2 * sub):
                halves = []
                for d in (0, sub):
                    row = pl.multiple_of(p * block + s + d, sub)
                    halves.append(
                        jnp.concatenate(
                            [
                                dx_ref[pl.ds(row, sub), j * lanes : (j + 1) * lanes]
                                for j in range(chunks)
                            ],
                            axis=0,
                        )
                    )
                tiles = jnp.dot(
                    swap_ref[...], jnp.concatenate(halves, axis=1), preferred_element_type=f32
                ).astype(bf16)
                for d in (0, 1):
                    e = b * block + s + d * sub
                    back_ref[e : e + sub, pl.ds(to, sub), :] = tiles[
                        :, d * lanes : (d + 1) * lanes
                    ].reshape(sub, sub, lanes)
            return carry

        lax.fori_loop(0, count, narrow, 0, unroll=True)

    for b in range(blocks):
        for i in range(5):
            out_copy(i, b).wait()


def expert_rows(wire, wg, wu, wd, start, count, block, carry=None):
    sources = wire.shape[0]
    width, hidden = wg.shape
    mine = sources * count
    last = carry is not None
    total = sources * capacity
    anywhere = pl.BlockSpec(memory_space=pltpu.HBM)
    high = count * sub + (8 if last else 0)
    back_spec = pl.BlockSpec(
        (pl.Element(sources), pl.Element(high), pl.Element(lanes)),
        lambda i: (0, start * sub, 0),
    )
    out_shape = [
        jax.ShapeDtypeStruct((total, width), bf16),
        jax.ShapeDtypeStruct((total, width), bf16),
        jax.ShapeDtypeStruct((total, hidden), bf16),
        jax.ShapeDtypeStruct((total, hidden), bf16),
        jax.ShapeDtypeStruct((total, hidden), bf16),
        jax.ShapeDtypeStruct((sources, capacity * sub + 8, lanes), bf16),
    ]
    out_specs = [anywhere] * 5 + [back_spec]
    in_specs = [anywhere, pl.BlockSpec(memory_space=pltpu.VMEM), anywhere, anywhere]
    args = [wire, pltpu.with_memory_space_constraint(wg, pltpu.VMEM), wu, wd]
    aliases = {}
    if last:
        in_specs += [whole((sources, lanes))] + [anywhere] * 6
        args += [carry[6]] + list(carry[:6])
        aliases = {5 + i: i for i in range(6)}
    else:
        out_specs.append(whole((sources, lanes)))
        out_shape.append(jax.ShapeDtypeStruct((sources, lanes), f32))
    return pl.pallas_call(
        functools.partial(expert_kernel, start, count, block, last),
        grid=(1,),
        in_specs=in_specs,
        out_specs=out_specs,
        out_shape=out_shape,
        scratch_shapes=[
            pltpu.VMEM(wire.shape, bf16),
            pltpu.VMEM((width, hidden), bf16),
            pltpu.VMEM((hidden, width), bf16),
            pltpu.VMEM((mine, width), bf16),
            pltpu.VMEM((mine, width), bf16),
            pltpu.VMEM((mine, hidden), bf16),
            pltpu.VMEM((mine, hidden), bf16),
            pltpu.VMEM((mine, hidden), bf16),
            pltpu.VMEM((block * count, width), bf16),
            pltpu.VMEM((sub * sub, sub * sub), bf16),
            pltpu.SemaphoreType.DMA((sources // block, 2)),
            pltpu.SemaphoreType.DMA((2,)),
            pltpu.SemaphoreType.DMA((5, sources // block)),
        ],
        input_output_aliases=aliases,
        compiler_params=params(60),
        cost_estimate=pl.CostEstimate(
            flops=10 * mine * width * hidden,
            bytes_accessed=6 * width * hidden + 12 * mine * width,
            transcendentals=mine * hidden,
        ),
        name="expert_rows_last" if last else "expert_rows_first",
    )(*args)


def combine_kernel(code_s_ref, code_ref, num_ref, back_ref, tok_ref, gate_ref, tiles_ref):
    toks, width = tok_ref.shape
    top = code_ref.shape[0]
    chunks = width // lanes
    experts = back_ref.shape[0]

    def one(t, carry):
        total = None
        for k in range(top):
            code = code_s_ref[k, t]
            at = pl.multiple_of((code & 15) << 4, sub)
            row = back_ref[code >> 4, pl.ds(at, sub), :].astype(f32)
            total = row if total is None else total + row
        tiles_ref[t] = total.astype(bf16)
        return carry

    lax.fori_loop(0, toks, one, 0, unroll=8)
    swap = swap_matrix()
    for r in range(0, toks, 2 * sub):
        tiles = jnp.concatenate(
            [tiles_ref[r + d : r + d + sub].reshape(sub * sub, lanes) for d in (0, sub)], axis=1
        )
        flat = jnp.dot(swap, tiles, preferred_element_type=f32).astype(bf16)
        for d in (0, 1):
            for j in range(chunks):
                tok_ref[r + d * sub : r + (d + 1) * sub, j * lanes : (j + 1) * lanes] = flat[
                    j * sub : (j + 1) * sub, d * lanes : (d + 1) * lanes
                ]

    grads = jnp.max(back_ref[:, capacity * sub : capacity * sub + 8, :].astype(f32), axis=1)
    grads = jnp.transpose(grads).astype(bf16)
    gate = num_ref[...].astype(f32) * (1.0 / 256.0)
    expert_at = lax.broadcasted_iota(jnp.int32, (experts, toks), 0)
    place_at = lax.broadcasted_iota(jnp.int32, (lanes, toks), 0)
    found = []
    for k in range(top):
        code = code_ref[k : k + 1, :]
        hit = jnp.where((code >> 4) == expert_at, 1.0, 0.0).astype(bf16)
        rows = jnp.dot(grads, hit, preferred_element_type=f32)
        found.append(jnp.sum(jnp.where((code & 15) == place_at, rows, 0.0), axis=0, keepdims=True))
    gate_ref[...] = (jnp.concatenate(found, axis=0) / gate).astype(bf16)


def combine(code, num, back, toks, width):
    top = code.shape[0]
    vmem = pl.BlockSpec(memory_space=pltpu.VMEM)
    return pl.pallas_call(
        combine_kernel,
        in_specs=[pl.BlockSpec(memory_space=pltpu.SMEM), vmem, vmem, vmem],
        out_specs=[vmem] * 2,
        out_shape=[
            jax.ShapeDtypeStruct((toks, width), bf16),
            jax.ShapeDtypeStruct((top, toks), bf16),
        ],
        scratch_shapes=[pltpu.VMEM((toks, width // lanes, lanes), bf16)],
        compiler_params=params(60),
        name="combine_rows",
    )(code, code, num, back)


def exchange(rows):
    return lax.all_to_all(rows, ("dp", "expert"), split_axis=0, concat_axis=0, tiled=True)


def local(tokens, d_out, expert_ids, gate_num, w_gate, w_up, w_down):
    toks, width = tokens.shape
    experts = lax.axis_size("dp") * lax.axis_size("expert")
    wg, wu, wd = w_gate[0], w_up[0], w_down[0]
    ids, num = expert_ids.T, gate_num.T
    rest = capacity - first_rows
    first, index, scale, code = pack(tokens, d_out, 0, first_rows, experts, ids, num)
    (second,) = pack(tokens, d_out, first_rows, rest, experts, tables=(index, scale))
    first, second = exchange(first), exchange(second)
    part = expert_rows(first, wg, wu, wd, 0, first_rows, 64)
    rows_x, rows_dy, h, da, db, back = expert_rows(second, wg, wu, wd, first_rows, rest, 128, part)
    back = exchange(back)
    grad_gate = lax.dot_general(rows_x, da, contract_rows, preferred_element_type=f32).astype(bf16)
    grad_up = lax.dot_general(rows_x, db, contract_rows, preferred_element_type=f32).astype(bf16)
    grad_down = lax.dot_general(h, rows_dy, contract_rows, preferred_element_type=f32).astype(bf16)
    d_tokens, d_gate = combine(code, num, back, toks, width)
    return (d_tokens, d_gate.T, grad_gate[None], grad_up[None], grad_down[None])


def solution(mesh):
    rows = P(("dp", "expert"), None)
    blocks = P(("dp", "expert"), None, None)
    return jax.shard_map(
        local,
        mesh=mesh,
        in_specs=(rows, rows, rows, rows, blocks, blocks, blocks),
        out_specs=(rows, rows, blocks, blocks, blocks),
        check_vma=False,
    )
```

```python
import functools

import jax
import jax.numpy as jnp
from jax import lax
from jax.experimental import pallas as pl
from jax.experimental.pallas import tpu as pltpu
from jax.sharding import PartitionSpec as P

bf16 = jnp.bfloat16
f32 = jnp.float32
lanes = 128
sub = 16
capacity = 9
first_rows = 7
contract_rows = (((0,), (0,)), ((), ()))
contract_cols = (((1,), (1,)), ((), ()))


def params(mib):
    return pltpu.CompilerParams(vmem_limit_bytes=mib * 1024 * 1024)


def whole(shape):
    return pl.BlockSpec(shape, lambda *_: (0,) * len(shape))


def swap_matrix():
    size = sub * sub
    row = lax.broadcasted_iota(jnp.int32, (size, size), 0)
    col = lax.broadcasted_iota(jnp.int32, (size, size), 1)
    return jnp.where(((row & 15) << 4) + (row >> 4) == col, 1.0, 0.0).astype(bf16)


def spread_tables(ids, num, experts):
    top, toks = ids.shape
    gate = num.astype(f32) * (1.0 / 256.0)
    expert_at = lax.broadcasted_iota(jnp.int32, (experts, toks), 0)
    named = jnp.zeros((experts, toks), f32)
    gates = jnp.zeros((experts, toks), f32)
    for k in range(top):
        hit = ids[k : k + 1, :] == expert_at
        named = jnp.where(hit, 1.0, named)
        gates = jnp.where(hit, gate[k : k + 1, :], gates)
    row = lax.broadcasted_iota(jnp.int32, (toks, toks), 0)
    col = lax.broadcasted_iota(jnp.int32, (toks, toks), 1)
    before = jnp.where(row < col, 1.0, 0.0).astype(bf16)
    place = jnp.dot(named.astype(bf16), before, preferred_element_type=f32)
    token = lax.broadcasted_iota(jnp.int32, (experts, toks), 1).astype(f32)
    here = [(named > 0.0) & (place == float(p)) for p in range(capacity)]
    wanted = lax.broadcasted_iota(jnp.int32, (sub, capacity * toks), 0)
    owner = lax.broadcasted_iota(jnp.int32, (sub, capacity * toks), 1) >> 7
    collect = jnp.where(owner == wanted, 1.0, 0.0).astype(bf16)
    index, scale = [
        lax.dot_general(
            collect,
            jnp.concatenate([jnp.where(h, v, 0.0).astype(bf16) for h in here], axis=1),
            contract_cols,
            preferred_element_type=f32,
        )
        for v in (token, gates)
    ]
    code = (expert_at * sub).astype(f32) + place
    spot = (expert_at * (capacity * sub)).astype(f32) + place * float(sub)
    codes, spots = [
        jnp.concatenate(
            [
                jnp.sum(jnp.where(ids[k : k + 1, :] == expert_at, v, 0.0), axis=0, keepdims=True)
                for k in range(top)
            ],
            axis=0,
        ).astype(jnp.int32)
        for v in (code, spot)
    ]
    return index.astype(jnp.int32), scale, codes, spots


def wide_to_tiles(swap, wide, chunks, store):
    rows = wide.shape[0]
    for r in range(0, rows, 2 * sub):
        halves = [
            jnp.concatenate(
                [wide[r + d : r + d + sub, j * lanes : (j + 1) * lanes] for j in range(chunks)], axis=0
            )
            for d in (0, sub)
        ]
        tiles = jnp.dot(swap, jnp.concatenate(halves, axis=1), preferred_element_type=f32)
        store(r, tiles[:, :lanes].reshape(sub, chunks, lanes))
        store(r + sub, tiles[:, lanes:].reshape(sub, chunks, lanes))


def make_tiles(tok_ref, dy_ref, tok_tiles, dy_tiles):
    swap = swap_matrix()
    chunks = tok_ref.shape[1] // lanes

    def put_tok(r, tiles):
        tok_tiles[r : r + sub] = tiles.astype(bf16)

    def put_dy(r, tiles):
        dy_tiles[r : r + sub] = tiles

    wide_to_tiles(swap, tok_ref, chunks, put_tok)
    wide_to_tiles(swap, dy_ref, chunks, put_dy)


def fill_rows(start, count, index_ref, scale_ref, tok_tiles, dy_tiles, buffer, out_hbm, sems):
    experts = buffer.shape[0]
    groups = sems.shape[0]
    group = experts // groups

    def out_copy(g):
        at = slice(g * group, (g + 1) * group)
        return pltpu.make_async_copy(buffer.at[at], out_hbm.at[at], sems.at[g])

    def one(e, carry):
        for p in range(count):
            token = index_ref[start + p, e]
            scale = scale_ref[start + p, e]
            buffer[e, p * sub : (p + 1) * sub, :] = tok_tiles[token]
            at = (count + p) * sub
            buffer[e, at : at + sub, :] = (dy_tiles[token] * scale).astype(bf16)
        return carry

    for g in range(groups):
        lax.fori_loop(g * group, (g + 1) * group, one, 0, unroll=2)
        out_copy(g).start()
    for g in range(groups):
        out_copy(g).wait()


def pack_first_kernel(
    start, count, ids_ref, num_ref, tok_ref, dy_ref,
    out_hbm, index_ref, scale_ref, code_ref, spot_ref,
    tok_tiles, dy_tiles, buffer, out_sems, index_s, scale_s, sems,
):
    index, scale, code, spot = spread_tables(ids_ref[...], num_ref[...], index_ref.shape[1])
    index_ref[...] = index
    scale_ref[...] = scale
    code_ref[...] = code
    spot_ref[...] = spot
    one = pltpu.make_async_copy(index_ref, index_s, sems.at[0])
    two = pltpu.make_async_copy(scale_ref, scale_s, sems.at[1])
    one.start()
    two.start()
    make_tiles(tok_ref, dy_ref, tok_tiles, dy_tiles)
    one.wait()
    two.wait()
    fill_rows(start, count, index_s, scale_s, tok_tiles, dy_tiles, buffer, out_hbm, out_sems)


def pack_rest_kernel(
    start, count, index_ref, scale_ref, tok_ref, dy_ref,
    out_hbm, tok_tiles, dy_tiles, buffer, out_sems,
):
    make_tiles(tok_ref, dy_ref, tok_tiles, dy_tiles)
    fill_rows(start, count, index_ref, scale_ref, tok_tiles, dy_tiles, buffer, out_hbm, out_sems)


def pack(tokens, d_out, start, count, experts, ids=None, num=None, tables=None):
    toks, width = tokens.shape
    chunks = width // lanes
    wire = (experts, 2 * count * sub, lanes)
    out_shape = [jax.ShapeDtypeStruct(wire, bf16)]
    out_specs = [pl.BlockSpec(memory_space=pl.ANY)]
    scratch = [
        pltpu.VMEM((toks, chunks, lanes), bf16),
        pltpu.VMEM((toks, chunks, lanes), f32),
        pltpu.VMEM(wire, bf16),
        pltpu.SemaphoreType.DMA((8,)),
    ]
    vmem = pl.BlockSpec(memory_space=pltpu.VMEM)
    if tables is None:
        body = functools.partial(pack_first_kernel, start, count)
        args = (ids, num, tokens, d_out)
        in_specs = [vmem] * 4
        out_shape += [
            jax.ShapeDtypeStruct((sub, experts), jnp.int32),
            jax.ShapeDtypeStruct((sub, experts), f32),
            jax.ShapeDtypeStruct(ids.shape, jnp.int32),
            jax.ShapeDtypeStruct(ids.shape, jnp.int32),
        ]
        out_specs += [vmem] * 4
        scratch += [
            pltpu.SMEM((sub, experts), jnp.int32),
            pltpu.SMEM((sub, experts), f32),
            pltpu.SemaphoreType.DMA((2,)),
        ]
    else:
        body = functools.partial(pack_rest_kernel, start, count)
        args = (*tables, tokens, d_out)
        in_specs = [pl.BlockSpec(memory_space=pltpu.SMEM)] * 2 + [vmem] * 2
    return pl.pallas_call(
        body,
        in_specs=in_specs,
        out_specs=out_specs,
        out_shape=out_shape,
        scratch_shapes=scratch,
        compiler_params=params(60),
        cost_estimate=pl.CostEstimate(
            flops=0, bytes_accessed=4 * experts * count * width, transcendentals=0
        ),
        name="pack_first" if tables is None else "pack_rest",
    )(*args)


def expert_kernel(start, count, block, last, *refs):
    (wire_hbm, wg, wu_hbm, wd_hbm) = refs[:4]
    refs = refs[4:]
    if last:
        old_gate_ref = refs[0]
        refs = refs[7:]
    out_hbm = refs[:5]
    back_ref = refs[5]
    refs = refs[6:]
    if not last:
        gate_ref = refs[0]
        refs = refs[1:]
    (wire, wu, wd, x_ref, dy_ref, h_ref, da_ref, db_ref, dx_ref, swap_ref) = refs[:10]
    (wire_sem, weight_sem, out_sem) = refs[10:]
    sources = wire_hbm.shape[0]
    blocks = sources // block
    rows = block * count
    width, hidden = wg.shape
    chunks = width // lanes
    part = 256
    half = count * sub

    def wire_copy(b, side):
        at = (slice(b * block, (b + 1) * block), slice(side * half, (side + 1) * half))
        return pltpu.make_async_copy(wire_hbm.at[at], wire.at[at], wire_sem.at[b, side])

    weights = [
        pltpu.make_async_copy(src, dst, weight_sem.at[i])
        for i, (src, dst) in enumerate(((wu_hbm, wu), (wd_hbm, wd)))
    ]

    def out_copy(i, b):
        src = (x_ref, dy_ref, h_ref, da_ref, db_ref)[i]
        to = sources * start + b * rows
        return pltpu.make_async_copy(
            src.at[b * rows : (b + 1) * rows], out_hbm[i].at[to : to + rows], out_sem.at[i, b]
        )

    wire_copy(0, 0).start()
    weights[0].start()
    wire_copy(0, 1).start()
    weights[1].start()
    for b in range(1, blocks):
        wire_copy(b, 0).start()
        wire_copy(b, 1).start()
    swap_ref[...] = swap_matrix()

    def widen(b, side, out):
        def step(p, carry):
            at = pl.multiple_of(side * half + p * sub, sub)
            for s in range(0, block, 2 * sub):
                tiles = jnp.concatenate(
                    [
                        wire[b * block + s + d : b * block + s + d + sub, pl.ds(at, sub), :].reshape(
                            sub * sub, lanes
                        )
                        for d in (0, sub)
                    ],
                    axis=1,
                )
                flat = jnp.dot(swap_ref[...], tiles, preferred_element_type=f32).astype(bf16)
                for d in (0, 1):
                    to = pl.multiple_of(b * rows + p * block + s + d * sub, sub)
                    for j in range(chunks):
                        out[pl.ds(to, sub), j * lanes : (j + 1) * lanes] = flat[
                            j * sub : (j + 1) * sub, d * lanes : (d + 1) * lanes
                        ]
            return carry

        lax.fori_loop(0, count, step, 0, unroll=True)

    for b in range(blocks):
        low, high = b * rows, (b + 1) * rows
        wire_copy(b, 0).wait()
        widen(b, 0, x_ref)
        out_copy(0, b).start()
        gates_in = [
            jnp.dot(x_ref[low:high], wg[:, n : n + part], preferred_element_type=f32)
            for n in range(0, hidden, part)
        ]
        wire_copy(b, 1).wait()
        widen(b, 1, dy_ref)
        out_copy(1, b).start()
        if b == 0:
            for copy in weights:
                copy.wait()

        gate_grad = jnp.zeros((rows, 1), f32)
        for n in range(0, hidden, part):
            x = x_ref[low:high]
            a = gates_in[n // part]
            up = jnp.dot(x, wu[:, n : n + part], preferred_element_type=f32)
            u = lax.dot_general(
                dy_ref[low:high], wd[n : n + part, :], contract_cols, preferred_element_type=f32
            )
            sig = jax.nn.sigmoid(a)
            active = a * sig
            h = active * up
            gate_grad = gate_grad + jnp.sum(u * h, axis=1, keepdims=True)
            h_ref[low:high, n : n + part] = h.astype(bf16)
            da_ref[low:high, n : n + part] = (u * up * sig * (1.0 + a * (1.0 - sig))).astype(bf16)
            db_ref[low:high, n : n + part] = (u * active).astype(bf16)
        for i in (2, 3, 4):
            out_copy(i, b).start()

        lane = lax.broadcasted_iota(jnp.int32, (block, lanes), 1)
        at = slice(b * block, (b + 1) * block)
        gates = old_gate_ref[at, :] if last else jnp.zeros((block, lanes), f32)
        for p in range(count):
            gates = jnp.where(lane == start + p, gate_grad[p * block : (p + 1) * block], gates)
        if last:
            eight = jnp.broadcast_to(gates[:, None, :], (block, 8, lanes))
            back_ref[at, half : half + 8, :] = eight.astype(bf16)
        else:
            gate_ref[at, :] = gates

        for n in range(0, width, part):
            dx = lax.dot_general(
                da_ref[low:high], wg[n : n + part, :], contract_cols, preferred_element_type=f32
            )
            dx = dx + lax.dot_general(
                db_ref[low:high], wu[n : n + part, :], contract_cols, preferred_element_type=f32
            )
            dx_ref[:, n : n + part] = dx.astype(bf16)

        def narrow(p, carry):
            to = pl.multiple_of(p * sub, sub)
            for s in range(0, block, 2 * sub):
                halves = []
                for d in (0, sub):
                    row = pl.multiple_of(p * block + s + d, sub)
                    halves.append(
                        jnp.concatenate(
                            [
                                dx_ref[pl.ds(row, sub), j * lanes : (j + 1) * lanes]
                                for j in range(chunks)
                            ],
                            axis=0,
                        )
                    )
                tiles = jnp.dot(
                    swap_ref[...], jnp.concatenate(halves, axis=1), preferred_element_type=f32
                ).astype(bf16)
                for d in (0, 1):
                    e = b * block + s + d * sub
                    back_ref[e : e + sub, pl.ds(to, sub), :] = tiles[
                        :, d * lanes : (d + 1) * lanes
                    ].reshape(sub, sub, lanes)
            return carry

        lax.fori_loop(0, count, narrow, 0, unroll=True)

    for b in range(blocks):
        for i in range(5):
            out_copy(i, b).wait()


def expert_rows(wire, wg, wu, wd, start, count, block, carry=None):
    sources = wire.shape[0]
    width, hidden = wg.shape
    mine = sources * count
    last = carry is not None
    total = sources * capacity
    anywhere = pl.BlockSpec(memory_space=pltpu.HBM)
    high = count * sub + (8 if last else 0)
    back_spec = pl.BlockSpec(
        (pl.Element(sources), pl.Element(high), pl.Element(lanes)),
        lambda i: (0, start * sub, 0),
    )
    out_shape = [
        jax.ShapeDtypeStruct((total, width), bf16),
        jax.ShapeDtypeStruct((total, width), bf16),
        jax.ShapeDtypeStruct((total, hidden), bf16),
        jax.ShapeDtypeStruct((total, hidden), bf16),
        jax.ShapeDtypeStruct((total, hidden), bf16),
        jax.ShapeDtypeStruct((sources, capacity * sub + 8, lanes), bf16),
    ]
    out_specs = [anywhere] * 5 + [back_spec]
    in_specs = [anywhere, pl.BlockSpec(memory_space=pltpu.VMEM), anywhere, anywhere]
    args = [wire, pltpu.with_memory_space_constraint(wg, pltpu.VMEM), wu, wd]
    aliases = {}
    if last:
        in_specs += [whole((sources, lanes))] + [anywhere] * 6
        args += [carry[6]] + list(carry[:6])
        aliases = {5 + i: i for i in range(6)}
    else:
        out_specs.append(whole((sources, lanes)))
        out_shape.append(jax.ShapeDtypeStruct((sources, lanes), f32))
    return pl.pallas_call(
        functools.partial(expert_kernel, start, count, block, last),
        grid=(1,),
        in_specs=in_specs,
        out_specs=out_specs,
        out_shape=out_shape,
        scratch_shapes=[
            pltpu.VMEM(wire.shape, bf16),
            pltpu.VMEM((width, hidden), bf16),
            pltpu.VMEM((hidden, width), bf16),
            pltpu.VMEM((mine, width), bf16),
            pltpu.VMEM((mine, width), bf16),
            pltpu.VMEM((mine, hidden), bf16),
            pltpu.VMEM((mine, hidden), bf16),
            pltpu.VMEM((mine, hidden), bf16),
            pltpu.VMEM((block * count, width), bf16),
            pltpu.VMEM((sub * sub, sub * sub), bf16),
            pltpu.SemaphoreType.DMA((sources // block, 2)),
            pltpu.SemaphoreType.DMA((2,)),
            pltpu.SemaphoreType.DMA((5, sources // block)),
        ],
        input_output_aliases=aliases,
        compiler_params=params(60),
        cost_estimate=pl.CostEstimate(
            flops=10 * mine * width * hidden,
            bytes_accessed=6 * width * hidden + 12 * mine * width,
            transcendentals=mine * hidden,
        ),
        name="expert_rows_last" if last else "expert_rows_first",
    )(*args)


def combine_kernel(spot_ref, code_ref, num_ref, back_ref, side_ref, tok_ref, gate_ref, tiles_ref):
    toks, width = tok_ref.shape
    top = code_ref.shape[0]
    chunks = width // lanes
    experts = back_ref.shape[0]
    flat_ref = back_ref.reshape(experts * capacity * sub, lanes)

    def one(t, carry):
        total = None
        for k in range(top):
            at = pl.multiple_of(spot_ref[k, t], sub)
            row = flat_ref[pl.ds(at, sub), :].astype(f32)
            total = row if total is None else total + row
        tiles_ref[t] = total.astype(bf16)
        return carry

    lax.fori_loop(0, toks, one, 0, unroll=8)
    swap = swap_matrix()
    for r in range(0, toks, 2 * sub):
        tiles = jnp.concatenate(
            [tiles_ref[r + d : r + d + sub].reshape(sub * sub, lanes) for d in (0, sub)], axis=1
        )
        flat = jnp.dot(swap, tiles, preferred_element_type=f32).astype(bf16)
        for d in (0, 1):
            for j in range(chunks):
                tok_ref[r + d * sub : r + (d + 1) * sub, j * lanes : (j + 1) * lanes] = flat[
                    j * sub : (j + 1) * sub, d * lanes : (d + 1) * lanes
                ]

    grads = jnp.max(side_ref[...].astype(f32), axis=1)
    grads = jnp.transpose(grads).astype(bf16)
    gate = num_ref[...].astype(f32) * (1.0 / 256.0)
    expert_at = lax.broadcasted_iota(jnp.int32, (experts, toks), 0)
    place_at = lax.broadcasted_iota(jnp.int32, (lanes, toks), 0)
    found = []
    for k in range(top):
        code = code_ref[k : k + 1, :]
        hit = jnp.where((code >> 4) == expert_at, 1.0, 0.0).astype(bf16)
        rows = jnp.dot(grads, hit, preferred_element_type=f32)
        found.append(jnp.sum(jnp.where((code & 15) == place_at, rows, 0.0), axis=0, keepdims=True))
    gate_ref[...] = (jnp.concatenate(found, axis=0) / gate).astype(bf16)


def combine(spot, code, num, back, toks, width):
    top = code.shape[0]
    experts = back.shape[0]

    def rows_of(at, count):
        return pl.BlockSpec(
            (pl.Element(experts), pl.Element(count), pl.Element(lanes)), lambda i: (0, at, 0)
        )

    return pl.pallas_call(
        combine_kernel,
        grid=(1,),
        in_specs=[
            pl.BlockSpec(memory_space=pltpu.SMEM),
            whole(code.shape),
            whole(num.shape),
            rows_of(0, capacity * sub),
            rows_of(capacity * sub, 8),
        ],
        out_specs=[whole((toks, width)), whole((top, toks))],
        out_shape=[
            jax.ShapeDtypeStruct((toks, width), bf16),
            jax.ShapeDtypeStruct((top, toks), bf16),
        ],
        scratch_shapes=[pltpu.VMEM((toks, width // lanes, lanes), bf16)],
        compiler_params=params(60),
        name="combine_rows",
    )(spot, code, num, back, back)


def exchange(rows):
    return lax.all_to_all(rows, ("dp", "expert"), split_axis=0, concat_axis=0, tiled=True)


def local(tokens, d_out, expert_ids, gate_num, w_gate, w_up, w_down):
    toks, width = tokens.shape
    experts = lax.axis_size("dp") * lax.axis_size("expert")
    wg, wu, wd = w_gate[0], w_up[0], w_down[0]
    ids, num = expert_ids.T, gate_num.T
    rest = capacity - first_rows
    first, index, scale, code, spot = pack(tokens, d_out, 0, first_rows, experts, ids, num)
    (second,) = pack(tokens, d_out, first_rows, rest, experts, tables=(index, scale))
    first, second = exchange(first), exchange(second)
    part = expert_rows(first, wg, wu, wd, 0, first_rows, 64)
    rows_x, rows_dy, h, da, db, back = expert_rows(second, wg, wu, wd, first_rows, rest, 128, part)
    back = exchange(back)
    grad_gate = lax.dot_general(rows_x, da, contract_rows, preferred_element_type=f32).astype(bf16)
    grad_up = lax.dot_general(rows_x, db, contract_rows, preferred_element_type=f32).astype(bf16)
    grad_down = lax.dot_general(h, rows_dy, contract_rows, preferred_element_type=f32).astype(bf16)
    d_tokens, d_gate = combine(spot, code, num, back, toks, width)
    return (d_tokens, d_gate.T, grad_gate[None], grad_up[None], grad_down[None])


def solution(mesh):
    rows = P(("dp", "expert"), None)
    blocks = P(("dp", "expert"), None, None)
    return jax.shard_map(
        local,
        mesh=mesh,
        in_specs=(rows, rows, rows, rows, blocks, blocks, blocks),
        out_specs=(rows, rows, blocks, blocks, blocks),
        check_vma=False,
    )
```

```python
import functools

import jax
import jax.numpy as jnp
from jax import lax
from jax.experimental import pallas as pl
from jax.experimental.pallas import tpu as pltpu
from jax.sharding import PartitionSpec as P

bf16 = jnp.bfloat16
f32 = jnp.float32
lanes = 128
sub = 16
capacity = 9
first_rows = 7
contract_rows = (((0,), (0,)), ((), ()))
contract_cols = (((1,), (1,)), ((), ()))


def params(mib):
    return pltpu.CompilerParams(vmem_limit_bytes=mib * 1024 * 1024)


def whole(shape):
    return pl.BlockSpec(shape, lambda *_: (0,) * len(shape))


def swap_matrix():
    size = sub * sub
    row = lax.broadcasted_iota(jnp.int32, (size, size), 0)
    col = lax.broadcasted_iota(jnp.int32, (size, size), 1)
    return jnp.where(((row & 15) << 4) + (row >> 4) == col, 1.0, 0.0).astype(bf16)


def spread_tables(ids, num, experts):
    top, toks = ids.shape
    gate = num.astype(f32) * (1.0 / 256.0)
    expert_at = lax.broadcasted_iota(jnp.int32, (experts, toks), 0)
    named = jnp.zeros((experts, toks), f32)
    gates = jnp.zeros((experts, toks), f32)
    for k in range(top):
        hit = ids[k : k + 1, :] == expert_at
        named = jnp.where(hit, 1.0, named)
        gates = jnp.where(hit, gate[k : k + 1, :], gates)
    row = lax.broadcasted_iota(jnp.int32, (toks, toks), 0)
    col = lax.broadcasted_iota(jnp.int32, (toks, toks), 1)
    before = jnp.where(row < col, 1.0, 0.0).astype(bf16)
    place = jnp.dot(named.astype(bf16), before, preferred_element_type=f32)
    token = lax.broadcasted_iota(jnp.int32, (experts, toks), 1).astype(f32)
    here = [(named > 0.0) & (place == float(p)) for p in range(capacity)]
    wanted = lax.broadcasted_iota(jnp.int32, (sub, capacity * toks), 0)
    owner = lax.broadcasted_iota(jnp.int32, (sub, capacity * toks), 1) >> 7
    collect = jnp.where(owner == wanted, 1.0, 0.0).astype(bf16)
    index, scale = [
        lax.dot_general(
            collect,
            jnp.concatenate([jnp.where(h, v, 0.0).astype(bf16) for h in here], axis=1),
            contract_cols,
            preferred_element_type=f32,
        )
        for v in (token, gates)
    ]
    code = (expert_at * sub).astype(f32) + place
    spot = (expert_at * (capacity * sub)).astype(f32) + place * float(sub)
    codes, spots = [
        jnp.concatenate(
            [
                jnp.sum(jnp.where(ids[k : k + 1, :] == expert_at, v, 0.0), axis=0, keepdims=True)
                for k in range(top)
            ],
            axis=0,
        ).astype(jnp.int32)
        for v in (code, spot)
    ]
    return index.astype(jnp.int32), scale, codes, spots


def wide_to_tiles(swap, wide, chunks, store):
    rows = wide.shape[0]
    for r in range(0, rows, 2 * sub):
        halves = [
            jnp.concatenate(
                [wide[r + d : r + d + sub, j * lanes : (j + 1) * lanes] for j in range(chunks)], axis=0
            )
            for d in (0, sub)
        ]
        tiles = jnp.dot(swap, jnp.concatenate(halves, axis=1), preferred_element_type=f32)
        store(r, tiles[:, :lanes].reshape(sub, chunks, lanes))
        store(r + sub, tiles[:, lanes:].reshape(sub, chunks, lanes))


def make_tiles(tok_ref, dy_ref, tok_tiles, dy_tiles):
    swap = swap_matrix()
    chunks = tok_ref.shape[1] // lanes

    def put_tok(r, tiles):
        tok_tiles[r : r + sub] = tiles.astype(bf16)

    def put_dy(r, tiles):
        dy_tiles[r : r + sub] = tiles

    wide_to_tiles(swap, tok_ref, chunks, put_tok)
    wide_to_tiles(swap, dy_ref, chunks, put_dy)


def fill_rows(start, count, index_ref, scale_ref, tok_tiles, dy_tiles, buffer, out_hbm, sems):
    experts = buffer.shape[0]
    groups = sems.shape[0]
    group = experts // groups

    def out_copy(g):
        at = slice(g * group, (g + 1) * group)
        return pltpu.make_async_copy(buffer.at[at], out_hbm.at[at], sems.at[g])

    def one(e, carry):
        for p in range(count):
            token = index_ref[start + p, e]
            scale = scale_ref[start + p, e]
            buffer[e, p * sub : (p + 1) * sub, :] = tok_tiles[token]
            at = (count + p) * sub
            buffer[e, at : at + sub, :] = (dy_tiles[token] * scale).astype(bf16)
        return carry

    for g in range(groups):
        lax.fori_loop(g * group, (g + 1) * group, one, 0, unroll=2)
        out_copy(g).start()
    for g in range(groups):
        out_copy(g).wait()


def pack_first_kernel(
    start, count, ids_ref, num_ref, tok_hbm, dy_hbm,
    out_hbm, index_ref, scale_ref, code_ref, spot_ref,
    tok_tiles, dy_tiles, buffer, out_sems, index_s, scale_s, tok_ref, dy_ref, sems,
):
    tok_in = pltpu.make_async_copy(tok_hbm, tok_ref, sems.at[2])
    dy_in = pltpu.make_async_copy(dy_hbm, dy_ref, sems.at[3])
    tok_in.start()
    dy_in.start()
    index, scale, code, spot = spread_tables(ids_ref[...], num_ref[...], index_ref.shape[1])
    index_ref[...] = index
    scale_ref[...] = scale
    one = pltpu.make_async_copy(index_ref, index_s, sems.at[0])
    two = pltpu.make_async_copy(scale_ref, scale_s, sems.at[1])
    one.start()
    two.start()
    code_ref[...] = code
    spot_ref[...] = spot
    tok_in.wait()
    dy_in.wait()
    make_tiles(tok_ref, dy_ref, tok_tiles, dy_tiles)
    one.wait()
    two.wait()
    fill_rows(start, count, index_s, scale_s, tok_tiles, dy_tiles, buffer, out_hbm, out_sems)


def pack_rest_kernel(
    start, count, index_ref, scale_ref, tok_ref, dy_ref,
    out_hbm, tok_tiles, dy_tiles, buffer, out_sems,
):
    make_tiles(tok_ref, dy_ref, tok_tiles, dy_tiles)
    fill_rows(start, count, index_ref, scale_ref, tok_tiles, dy_tiles, buffer, out_hbm, out_sems)


def pack(tokens, d_out, start, count, experts, ids=None, num=None, tables=None):
    toks, width = tokens.shape
    chunks = width // lanes
    wire = (experts, 2 * count * sub, lanes)
    out_shape = [jax.ShapeDtypeStruct(wire, bf16)]
    out_specs = [pl.BlockSpec(memory_space=pl.ANY)]
    scratch = [
        pltpu.VMEM((toks, chunks, lanes), bf16),
        pltpu.VMEM((toks, chunks, lanes), f32),
        pltpu.VMEM(wire, bf16),
        pltpu.SemaphoreType.DMA((8,)),
    ]
    vmem = pl.BlockSpec(memory_space=pltpu.VMEM)
    if tables is None:
        body = functools.partial(pack_first_kernel, start, count)
        args = (ids, num, tokens, d_out)
        in_specs = [vmem] * 2 + [pl.BlockSpec(memory_space=pl.ANY)] * 2
        out_shape += [
            jax.ShapeDtypeStruct((sub, experts), jnp.int32),
            jax.ShapeDtypeStruct((sub, experts), f32),
            jax.ShapeDtypeStruct(ids.shape, jnp.int32),
            jax.ShapeDtypeStruct(ids.shape, jnp.int32),
        ]
        out_specs += [vmem] * 4
        scratch += [
            pltpu.SMEM((sub, experts), jnp.int32),
            pltpu.SMEM((sub, experts), f32),
            pltpu.VMEM(tokens.shape, bf16),
            pltpu.VMEM(d_out.shape, bf16),
            pltpu.SemaphoreType.DMA((4,)),
        ]
    else:
        body = functools.partial(pack_rest_kernel, start, count)
        args = (*tables, tokens, d_out)
        in_specs = [pl.BlockSpec(memory_space=pltpu.SMEM)] * 2 + [vmem] * 2
    return pl.pallas_call(
        body,
        in_specs=in_specs,
        out_specs=out_specs,
        out_shape=out_shape,
        scratch_shapes=scratch,
        compiler_params=params(60),
        cost_estimate=pl.CostEstimate(
            flops=0, bytes_accessed=4 * experts * count * width, transcendentals=0
        ),
        name="pack_first" if tables is None else "pack_rest",
    )(*args)


def expert_kernel(start, count, block, last, *refs):
    (wire_hbm, wg, wu_hbm, wd_hbm) = refs[:4]
    refs = refs[4:]
    if last:
        old_gate_hbm = refs[0]
        refs = refs[7:]
    out_hbm = refs[:5]
    back_ref = refs[5]
    refs = refs[6:]
    if not last:
        gate_ref = refs[0]
        refs = refs[1:]
    (wire, wu, wd, x_ref, dy_ref, h_ref, da_ref, db_ref, dx_ref, swap_ref) = refs[:10]
    (wire_sem, weight_sem, out_sem) = refs[10:13]
    if last:
        (old_gate_ref, old_gate_sem) = refs[13:]
        old_gate = pltpu.make_async_copy(old_gate_hbm, old_gate_ref, old_gate_sem)
    sources = wire_hbm.shape[0]
    blocks = sources // block
    rows = block * count
    width, hidden = wg.shape
    chunks = width // lanes
    part = 256
    half = count * sub

    def wire_copy(b, side):
        at = (slice(b * block, (b + 1) * block), slice(side * half, (side + 1) * half))
        return pltpu.make_async_copy(wire_hbm.at[at], wire.at[at], wire_sem.at[b, side])

    weights = [
        pltpu.make_async_copy(src, dst, weight_sem.at[i])
        for i, (src, dst) in enumerate(((wu_hbm, wu), (wd_hbm, wd)))
    ]

    def out_copy(i, b):
        src = (x_ref, dy_ref, h_ref, da_ref, db_ref)[i]
        to = sources * start + b * rows
        return pltpu.make_async_copy(
            src.at[b * rows : (b + 1) * rows], out_hbm[i].at[to : to + rows], out_sem.at[i, b]
        )

    wire_copy(0, 0).start()
    weights[0].start()
    wire_copy(0, 1).start()
    weights[1].start()
    for b in range(1, blocks):
        wire_copy(b, 0).start()
        wire_copy(b, 1).start()
    if last:
        old_gate.start()
    swap_ref[...] = swap_matrix()

    def widen(b, side, out):
        def step(p, carry):
            at = pl.multiple_of(side * half + p * sub, sub)
            for s in range(0, block, 2 * sub):
                tiles = jnp.concatenate(
                    [
                        wire[b * block + s + d : b * block + s + d + sub, pl.ds(at, sub), :].reshape(
                            sub * sub, lanes
                        )
                        for d in (0, sub)
                    ],
                    axis=1,
                )
                flat = jnp.dot(swap_ref[...], tiles, preferred_element_type=f32).astype(bf16)
                for d in (0, 1):
                    to = pl.multiple_of(b * rows + p * block + s + d * sub, sub)
                    for j in range(chunks):
                        out[pl.ds(to, sub), j * lanes : (j + 1) * lanes] = flat[
                            j * sub : (j + 1) * sub, d * lanes : (d + 1) * lanes
                        ]
            return carry

        lax.fori_loop(0, count, step, 0, unroll=True)

    for b in range(blocks):
        low, high = b * rows, (b + 1) * rows
        wire_copy(b, 0).wait()
        widen(b, 0, x_ref)
        out_copy(0, b).start()
        gates_in = [
            jnp.dot(x_ref[low:high], wg[:, n : n + part], preferred_element_type=f32)
            for n in range(0, hidden, part)
        ]
        wire_copy(b, 1).wait()
        widen(b, 1, dy_ref)
        out_copy(1, b).start()
        if b == 0:
            for copy in weights:
                copy.wait()

        gate_grad = jnp.zeros((rows, 1), f32)
        for n in range(0, hidden, part):
            x = x_ref[low:high]
            a = gates_in[n // part]
            up = jnp.dot(x, wu[:, n : n + part], preferred_element_type=f32)
            u = lax.dot_general(
                dy_ref[low:high], wd[n : n + part, :], contract_cols, preferred_element_type=f32
            )
            sig = jax.nn.sigmoid(a)
            active = a * sig
            h = active * up
            gate_grad = gate_grad + jnp.sum(u * h, axis=1, keepdims=True)
            h_ref[low:high, n : n + part] = h.astype(bf16)
            da_ref[low:high, n : n + part] = (u * up * sig * (1.0 + a * (1.0 - sig))).astype(bf16)
            db_ref[low:high, n : n + part] = (u * active).astype(bf16)
        for i in (2, 3, 4):
            out_copy(i, b).start()

        lane = lax.broadcasted_iota(jnp.int32, (block, lanes), 1)
        at = slice(b * block, (b + 1) * block)
        if last:
            old_gate.wait()
        gates = old_gate_ref[at, :] if last else jnp.zeros((block, lanes), f32)
        for p in range(count):
            gates = jnp.where(lane == start + p, gate_grad[p * block : (p + 1) * block], gates)
        if last:
            eight = jnp.broadcast_to(gates[:, None, :], (block, 8, lanes))
            back_ref[at, half : half + 8, :] = eight.astype(bf16)
        else:
            gate_ref[at, :] = gates

        for n in range(0, width, part):
            dx = lax.dot_general(
                da_ref[low:high], wg[n : n + part, :], contract_cols, preferred_element_type=f32
            )
            dx = dx + lax.dot_general(
                db_ref[low:high], wu[n : n + part, :], contract_cols, preferred_element_type=f32
            )
            dx_ref[:, n : n + part] = dx.astype(bf16)

        def narrow(p, carry):
            to = pl.multiple_of(p * sub, sub)
            for s in range(0, block, 2 * sub):
                halves = []
                for d in (0, sub):
                    row = pl.multiple_of(p * block + s + d, sub)
                    halves.append(
                        jnp.concatenate(
                            [
                                dx_ref[pl.ds(row, sub), j * lanes : (j + 1) * lanes]
                                for j in range(chunks)
                            ],
                            axis=0,
                        )
                    )
                tiles = jnp.dot(
                    swap_ref[...], jnp.concatenate(halves, axis=1), preferred_element_type=f32
                ).astype(bf16)
                for d in (0, 1):
                    e = b * block + s + d * sub
                    back_ref[e : e + sub, pl.ds(to, sub), :] = tiles[
                        :, d * lanes : (d + 1) * lanes
                    ].reshape(sub, sub, lanes)
            return carry

        lax.fori_loop(0, count, narrow, 0, unroll=True)

    for b in range(blocks):
        for i in range(5):
            out_copy(i, b).wait()


def expert_rows(wire, wg, wu, wd, start, count, block, carry=None):
    sources = wire.shape[0]
    width, hidden = wg.shape
    mine = sources * count
    last = carry is not None
    total = sources * capacity
    anywhere = pl.BlockSpec(memory_space=pltpu.HBM)
    high = count * sub + (8 if last else 0)
    back_spec = pl.BlockSpec(
        (pl.Element(sources), pl.Element(high), pl.Element(lanes)),
        lambda i: (0, start * sub, 0),
    )
    out_shape = [
        jax.ShapeDtypeStruct((total, width), bf16),
        jax.ShapeDtypeStruct((total, width), bf16),
        jax.ShapeDtypeStruct((total, hidden), bf16),
        jax.ShapeDtypeStruct((total, hidden), bf16),
        jax.ShapeDtypeStruct((total, hidden), bf16),
        jax.ShapeDtypeStruct((sources, capacity * sub + 8, lanes), bf16),
    ]
    out_specs = [anywhere] * 5 + [back_spec]
    in_specs = [anywhere, pl.BlockSpec(memory_space=pltpu.VMEM), anywhere, anywhere]
    args = [wire, pltpu.with_memory_space_constraint(wg, pltpu.VMEM), wu, wd]
    aliases = {}
    if last:
        in_specs += [anywhere] * 7
        args += [carry[6]] + list(carry[:6])
        aliases = {5 + i: i for i in range(6)}
    else:
        out_specs.append(whole((sources, lanes)))
        out_shape.append(jax.ShapeDtypeStruct((sources, lanes), f32))
    scratch = []
    if last:
        scratch = [pltpu.VMEM((sources, lanes), f32), pltpu.SemaphoreType.DMA]
    return pl.pallas_call(
        functools.partial(expert_kernel, start, count, block, last),
        grid=(1,),
        in_specs=in_specs,
        out_specs=out_specs,
        out_shape=out_shape,
        scratch_shapes=[
            pltpu.VMEM(wire.shape, bf16),
            pltpu.VMEM((width, hidden), bf16),
            pltpu.VMEM((hidden, width), bf16),
            pltpu.VMEM((mine, width), bf16),
            pltpu.VMEM((mine, width), bf16),
            pltpu.VMEM((mine, hidden), bf16),
            pltpu.VMEM((mine, hidden), bf16),
            pltpu.VMEM((mine, hidden), bf16),
            pltpu.VMEM((block * count, width), bf16),
            pltpu.VMEM((sub * sub, sub * sub), bf16),
            pltpu.SemaphoreType.DMA((sources // block, 2)),
            pltpu.SemaphoreType.DMA((2,)),
            pltpu.SemaphoreType.DMA((5, sources // block)),
        ]
        + scratch,
        input_output_aliases=aliases,
        compiler_params=params(60),
        cost_estimate=pl.CostEstimate(
            flops=10 * mine * width * hidden,
            bytes_accessed=6 * width * hidden + 12 * mine * width,
            transcendentals=mine * hidden,
        ),
        name="expert_rows_last" if last else "expert_rows_first",
    )(*args)


def combine_kernel(spot_ref, code_ref, num_ref, back_ref, side_ref, tok_ref, gate_ref, tiles_ref):
    toks, width = tok_ref.shape
    top = code_ref.shape[0]
    chunks = width // lanes
    experts = back_ref.shape[0]
    flat_ref = back_ref.reshape(experts * capacity * sub, lanes)

    def one(t, carry):
        total = None
        for k in range(top):
            at = pl.multiple_of(spot_ref[k, t], sub)
            row = flat_ref[pl.ds(at, sub), :].astype(f32)
            total = row if total is None else total + row
        tiles_ref[t] = total.astype(bf16)
        return carry

    lax.fori_loop(0, toks, one, 0, unroll=8)
    swap = swap_matrix()
    for r in range(0, toks, 2 * sub):
        tiles = jnp.concatenate(
            [tiles_ref[r + d : r + d + sub].reshape(sub * sub, lanes) for d in (0, sub)], axis=1
        )
        flat = jnp.dot(swap, tiles, preferred_element_type=f32).astype(bf16)
        for d in (0, 1):
            for j in range(chunks):
                tok_ref[r + d * sub : r + (d + 1) * sub, j * lanes : (j + 1) * lanes] = flat[
                    j * sub : (j + 1) * sub, d * lanes : (d + 1) * lanes
                ]

    grads = jnp.max(side_ref[...].astype(f32), axis=1)
    grads = jnp.transpose(grads).astype(bf16)
    gate = num_ref[...].astype(f32) * (1.0 / 256.0)
    expert_at = lax.broadcasted_iota(jnp.int32, (experts, toks), 0)
    place_at = lax.broadcasted_iota(jnp.int32, (lanes, toks), 0)
    found = []
    for k in range(top):
        code = code_ref[k : k + 1, :]
        hit = jnp.where((code >> 4) == expert_at, 1.0, 0.0).astype(bf16)
        rows = jnp.dot(grads, hit, preferred_element_type=f32)
        found.append(jnp.sum(jnp.where((code & 15) == place_at, rows, 0.0), axis=0, keepdims=True))
    gate_ref[...] = (jnp.concatenate(found, axis=0) / gate).astype(bf16)


def combine(spot, code, num, back, toks, width):
    top = code.shape[0]
    experts = back.shape[0]

    def rows_of(at, count):
        return pl.BlockSpec(
            (pl.Element(experts), pl.Element(count), pl.Element(lanes)), lambda i: (0, at, 0)
        )

    return pl.pallas_call(
        combine_kernel,
        grid=(1,),
        in_specs=[
            pl.BlockSpec(memory_space=pltpu.SMEM),
            whole(code.shape),
            whole(num.shape),
            rows_of(0, capacity * sub),
            rows_of(capacity * sub, 8),
        ],
        out_specs=[whole((toks, width)), whole((top, toks))],
        out_shape=[
            jax.ShapeDtypeStruct((toks, width), bf16),
            jax.ShapeDtypeStruct((top, toks), bf16),
        ],
        scratch_shapes=[pltpu.VMEM((toks, width // lanes, lanes), bf16)],
        compiler_params=params(60),
        name="combine_rows",
    )(spot, code, num, back, back)


def exchange(rows):
    return lax.all_to_all(rows, ("dp", "expert"), split_axis=0, concat_axis=0, tiled=True)


def local(tokens, d_out, expert_ids, gate_num, w_gate, w_up, w_down):
    toks, width = tokens.shape
    experts = lax.axis_size("dp") * lax.axis_size("expert")
    wg, wu, wd = w_gate[0], w_up[0], w_down[0]
    ids, num = expert_ids.T, gate_num.T
    rest = capacity - first_rows
    first, index, scale, code, spot = pack(tokens, d_out, 0, first_rows, experts, ids, num)
    (second,) = pack(tokens, d_out, first_rows, rest, experts, tables=(index, scale))
    first, second = exchange(first), exchange(second)
    part = expert_rows(first, wg, wu, wd, 0, first_rows, 64)
    rows_x, rows_dy, h, da, db, back = expert_rows(second, wg, wu, wd, first_rows, rest, 128, part)
    back = exchange(back)
    grad_gate = lax.dot_general(rows_x, da, contract_rows, preferred_element_type=f32).astype(bf16)
    grad_up = lax.dot_general(rows_x, db, contract_rows, preferred_element_type=f32).astype(bf16)
    grad_down = lax.dot_general(h, rows_dy, contract_rows, preferred_element_type=f32).astype(bf16)
    d_tokens, d_gate = combine(spot, code, num, back, toks, width)
    return (d_tokens, d_gate.T, grad_gate[None], grad_up[None], grad_down[None])


def solution(mesh):
    rows = P(("dp", "expert"), None)
    blocks = P(("dp", "expert"), None, None)
    return jax.shard_map(
        local,
        mesh=mesh,
        in_specs=(rows, rows, rows, rows, blocks, blocks, blocks),
        out_specs=(rows, rows, blocks, blocks, blocks),
        check_vma=False,
    )
```

```python
import functools

import jax
import jax.numpy as jnp
from jax import lax
from jax.experimental import pallas as pl
from jax.experimental.pallas import tpu as pltpu
from jax.sharding import PartitionSpec as P

bf16 = jnp.bfloat16
f32 = jnp.float32
lanes = 128
sub = 16
capacity = 9
first_rows = 7
contract_rows = (((0,), (0,)), ((), ()))
contract_cols = (((1,), (1,)), ((), ()))


def params(mib):
    return pltpu.CompilerParams(vmem_limit_bytes=mib * 1024 * 1024)


def whole(shape):
    return pl.BlockSpec(shape, lambda *_: (0,) * len(shape))


def swap_matrix():
    size = sub * sub
    row = lax.broadcasted_iota(jnp.int32, (size, size), 0)
    col = lax.broadcasted_iota(jnp.int32, (size, size), 1)
    return jnp.where(((row & 15) << 4) + (row >> 4) == col, 1.0, 0.0).astype(bf16)


def spread_tables(ids, num, experts):
    top, toks = ids.shape
    gate = num.astype(f32) * (1.0 / 256.0)
    expert_at = lax.broadcasted_iota(jnp.int32, (experts, toks), 0)
    named = jnp.zeros((experts, toks), f32)
    gates = jnp.zeros((experts, toks), f32)
    for k in range(top):
        hit = ids[k : k + 1, :] == expert_at
        named = jnp.where(hit, 1.0, named)
        gates = jnp.where(hit, gate[k : k + 1, :], gates)
    row = lax.broadcasted_iota(jnp.int32, (toks, toks), 0)
    col = lax.broadcasted_iota(jnp.int32, (toks, toks), 1)
    before = jnp.where(row < col, 1.0, 0.0).astype(bf16)
    place = jnp.dot(named.astype(bf16), before, preferred_element_type=f32)
    token = lax.broadcasted_iota(jnp.int32, (experts, toks), 1).astype(f32)
    here = [(named > 0.0) & (place == float(p)) for p in range(capacity)]
    wanted = lax.broadcasted_iota(jnp.int32, (sub, capacity * toks), 0)
    owner = lax.broadcasted_iota(jnp.int32, (sub, capacity * toks), 1) >> 7
    collect = jnp.where(owner == wanted, 1.0, 0.0).astype(bf16)
    index, scale = [
        lax.dot_general(
            collect,
            jnp.concatenate([jnp.where(h, v, 0.0).astype(bf16) for h in here], axis=1),
            contract_cols,
            preferred_element_type=f32,
        )
        for v in (token, gates)
    ]
    code = (expert_at * sub).astype(f32) + place
    spot = (expert_at * (capacity * sub)).astype(f32) + place * float(sub)
    codes, spots = [
        jnp.concatenate(
            [
                jnp.sum(jnp.where(ids[k : k + 1, :] == expert_at, v, 0.0), axis=0, keepdims=True)
                for k in range(top)
            ],
            axis=0,
        ).astype(jnp.int32)
        for v in (code, spot)
    ]
    return index.astype(jnp.int32), scale, codes, spots


def wide_to_tiles(swap, wide, chunks, store):
    rows = wide.shape[0]
    for r in range(0, rows, 2 * sub):
        halves = [
            jnp.concatenate(
                [wide[r + d : r + d + sub, j * lanes : (j + 1) * lanes] for j in range(chunks)], axis=0
            )
            for d in (0, sub)
        ]
        tiles = jnp.dot(swap, jnp.concatenate(halves, axis=1), preferred_element_type=f32)
        store(r, tiles[:, :lanes].reshape(sub, chunks, lanes))
        store(r + sub, tiles[:, lanes:].reshape(sub, chunks, lanes))


def make_tiles(tok_ref, dy_ref, tok_tiles, dy_tiles):
    swap = swap_matrix()
    chunks = tok_ref.shape[1] // lanes

    def put_tok(r, tiles):
        tok_tiles[r : r + sub] = tiles.astype(bf16)

    def put_dy(r, tiles):
        dy_tiles[r : r + sub] = tiles

    wide_to_tiles(swap, tok_ref, chunks, put_tok)
    wide_to_tiles(swap, dy_ref, chunks, put_dy)


def fill_rows(start, count, index_ref, scale_ref, tok_tiles, dy_tiles, buffer, out_hbm, sems):
    experts = buffer.shape[0]
    groups = sems.shape[0]
    group = experts // groups

    def out_copy(g):
        at = slice(g * group, (g + 1) * group)
        return pltpu.make_async_copy(buffer.at[at], out_hbm.at[at], sems.at[g])

    def one(e, carry):
        for p in range(count):
            token = index_ref[start + p, e]
            scale = scale_ref[start + p, e]
            buffer[e, p * sub : (p + 1) * sub, :] = tok_tiles[token]
            at = (count + p) * sub
            buffer[e, at : at + sub, :] = (dy_tiles[token] * scale).astype(bf16)
        return carry

    for g in range(groups):
        lax.fori_loop(g * group, (g + 1) * group, one, 0, unroll=2)
        out_copy(g).start()
    for g in range(groups):
        out_copy(g).wait()


def pack_first_kernel(
    start, count, ids_ref, num_ref, tok_hbm, dy_hbm,
    out_hbm, index_ref, scale_ref, code_ref, spot_ref,
    tok_tiles, dy_tiles, buffer, out_sems, index_s, scale_s, tok_ref, dy_ref, sems,
):
    tok_in = pltpu.make_async_copy(tok_hbm, tok_ref, sems.at[2])
    dy_in = pltpu.make_async_copy(dy_hbm, dy_ref, sems.at[3])
    tok_in.start()
    dy_in.start()
    index, scale, code, spot = spread_tables(ids_ref[...], num_ref[...], index_ref.shape[1])
    index_ref[...] = index
    scale_ref[...] = scale
    one = pltpu.make_async_copy(index_ref, index_s, sems.at[0])
    two = pltpu.make_async_copy(scale_ref, scale_s, sems.at[1])
    one.start()
    two.start()
    code_ref[...] = code
    spot_ref[...] = spot
    tok_in.wait()
    dy_in.wait()
    make_tiles(tok_ref, dy_ref, tok_tiles, dy_tiles)
    one.wait()
    two.wait()
    fill_rows(start, count, index_s, scale_s, tok_tiles, dy_tiles, buffer, out_hbm, out_sems)


def pack_rest_kernel(
    start, count, index_ref, scale_ref, tok_ref, dy_ref,
    out_hbm, tok_tiles, dy_tiles, buffer, out_sems,
):
    make_tiles(tok_ref, dy_ref, tok_tiles, dy_tiles)
    fill_rows(start, count, index_ref, scale_ref, tok_tiles, dy_tiles, buffer, out_hbm, out_sems)


def pack(tokens, d_out, start, count, experts, ids=None, num=None, tables=None):
    toks, width = tokens.shape
    chunks = width // lanes
    wire = (experts, 2 * count * sub, lanes)
    out_shape = [jax.ShapeDtypeStruct(wire, bf16)]
    out_specs = [pl.BlockSpec(memory_space=pl.ANY)]
    scratch = [
        pltpu.VMEM((toks, chunks, lanes), bf16),
        pltpu.VMEM((toks, chunks, lanes), f32),
        pltpu.VMEM(wire, bf16),
        pltpu.SemaphoreType.DMA((16,)),
    ]
    vmem = pl.BlockSpec(memory_space=pltpu.VMEM)
    if tables is None:
        body = functools.partial(pack_first_kernel, start, count)
        args = (ids, num, tokens, d_out)
        in_specs = [vmem] * 2 + [pl.BlockSpec(memory_space=pl.ANY)] * 2
        out_shape += [
            jax.ShapeDtypeStruct((sub, experts), jnp.int32),
            jax.ShapeDtypeStruct((sub, experts), f32),
            jax.ShapeDtypeStruct(ids.shape, jnp.int32),
            jax.ShapeDtypeStruct(ids.shape, jnp.int32),
        ]
        out_specs += [vmem] * 4
        scratch += [
            pltpu.SMEM((sub, experts), jnp.int32),
            pltpu.SMEM((sub, experts), f32),
            pltpu.VMEM(tokens.shape, bf16),
            pltpu.VMEM(d_out.shape, bf16),
            pltpu.SemaphoreType.DMA((4,)),
        ]
    else:
        body = functools.partial(pack_rest_kernel, start, count)
        args = (*tables, tokens, d_out)
        in_specs = [pl.BlockSpec(memory_space=pltpu.SMEM)] * 2 + [vmem] * 2
    return pl.pallas_call(
        body,
        in_specs=in_specs,
        out_specs=out_specs,
        out_shape=out_shape,
        scratch_shapes=scratch,
        compiler_params=params(60),
        cost_estimate=pl.CostEstimate(
            flops=0, bytes_accessed=4 * experts * count * width, transcendentals=0
        ),
        name="pack_first" if tables is None else "pack_rest",
    )(*args)


def expert_kernel(start, count, block, last, *refs):
    (wire_hbm, wg, wu_hbm, wd_hbm) = refs[:4]
    refs = refs[4:]
    if last:
        old_gate_hbm = refs[0]
        refs = refs[7:]
    out_hbm = refs[:5]
    back_ref = refs[5]
    refs = refs[6:]
    if not last:
        gate_ref = refs[0]
        refs = refs[1:]
    (wire, wu, wd, x_ref, dy_ref, h_ref, da_ref, db_ref, dx_ref, swap_ref) = refs[:10]
    (wire_sem, weight_sem, out_sem) = refs[10:13]
    if last:
        (old_gate_ref, old_gate_sem) = refs[13:]
        old_gate = pltpu.make_async_copy(old_gate_hbm, old_gate_ref, old_gate_sem)
    sources = wire_hbm.shape[0]
    blocks = sources // block
    rows = block * count
    width, hidden = wg.shape
    chunks = width // lanes
    part = 256
    half = count * sub

    near = block // 2

    def wire_copy(b, side, piece):
        low = b * block + piece * near
        at = (slice(low, low + near), slice(side * half, (side + 1) * half))
        return pltpu.make_async_copy(wire_hbm.at[at], wire.at[at], wire_sem.at[b, side, piece])

    def wire_start(b, side):
        for piece in (0, 1):
            wire_copy(b, side, piece).start()

    weights = [
        pltpu.make_async_copy(src, dst, weight_sem.at[i])
        for i, (src, dst) in enumerate(((wu_hbm, wu), (wd_hbm, wd)))
    ]

    def out_copy(i, b):
        src = (x_ref, dy_ref, h_ref, da_ref, db_ref)[i]
        to = sources * start + b * rows
        return pltpu.make_async_copy(
            src.at[b * rows : (b + 1) * rows], out_hbm[i].at[to : to + rows], out_sem.at[i, b]
        )

    wire_start(0, 0)
    weights[0].start()
    wire_start(0, 1)
    weights[1].start()
    for b in range(1, blocks):
        wire_start(b, 0)
        wire_start(b, 1)
    if last:
        old_gate.start()
    swap_ref[...] = swap_matrix()

    def widen(b, side, piece, out):
        def step(p, carry):
            at = pl.multiple_of(side * half + p * sub, sub)
            for s in range(piece * near, (piece + 1) * near, 2 * sub):
                tiles = jnp.concatenate(
                    [
                        wire[b * block + s + d : b * block + s + d + sub, pl.ds(at, sub), :].reshape(
                            sub * sub, lanes
                        )
                        for d in (0, sub)
                    ],
                    axis=1,
                )
                flat = jnp.dot(swap_ref[...], tiles, preferred_element_type=f32).astype(bf16)
                for d in (0, 1):
                    to = pl.multiple_of(b * rows + p * block + s + d * sub, sub)
                    for j in range(chunks):
                        out[pl.ds(to, sub), j * lanes : (j + 1) * lanes] = flat[
                            j * sub : (j + 1) * sub, d * lanes : (d + 1) * lanes
                        ]
            return carry

        lax.fori_loop(0, count, step, 0, unroll=True)

    for b in range(blocks):
        low, high = b * rows, (b + 1) * rows
        for piece in (0, 1):
            wire_copy(b, 0, piece).wait()
            widen(b, 0, piece, x_ref)
        out_copy(0, b).start()
        gates_in = [
            jnp.dot(x_ref[low:high], wg[:, n : n + part], preferred_element_type=f32)
            for n in range(0, hidden, part)
        ]
        for piece in (0, 1):
            wire_copy(b, 1, piece).wait()
            widen(b, 1, piece, dy_ref)
        out_copy(1, b).start()
        if b == 0:
            for copy in weights:
                copy.wait()

        gate_grad = jnp.zeros((rows, 1), f32)
        for n in range(0, hidden, part):
            x = x_ref[low:high]
            a = gates_in[n // part]
            up = jnp.dot(x, wu[:, n : n + part], preferred_element_type=f32)
            u = lax.dot_general(
                dy_ref[low:high], wd[n : n + part, :], contract_cols, preferred_element_type=f32
            )
            sig = jax.nn.sigmoid(a)
            active = a * sig
            h = active * up
            gate_grad = gate_grad + jnp.sum(u * h, axis=1, keepdims=True)
            h_ref[low:high, n : n + part] = h.astype(bf16)
            da_ref[low:high, n : n + part] = (u * up * sig * (1.0 + a * (1.0 - sig))).astype(bf16)
            db_ref[low:high, n : n + part] = (u * active).astype(bf16)
        for i in (2, 3, 4):
            out_copy(i, b).start()

        lane = lax.broadcasted_iota(jnp.int32, (block, lanes), 1)
        at = slice(b * block, (b + 1) * block)
        if last:
            old_gate.wait()
        gates = old_gate_ref[at, :] if last else jnp.zeros((block, lanes), f32)
        for p in range(count):
            gates = jnp.where(lane == start + p, gate_grad[p * block : (p + 1) * block], gates)
        if last:
            eight = jnp.broadcast_to(gates[:, None, :], (block, 8, lanes))
            back_ref[at, half : half + 8, :] = eight.astype(bf16)
        else:
            gate_ref[at, :] = gates

        for n in range(0, width, part):
            dx = lax.dot_general(
                da_ref[low:high], wg[n : n + part, :], contract_cols, preferred_element_type=f32
            )
            dx = dx + lax.dot_general(
                db_ref[low:high], wu[n : n + part, :], contract_cols, preferred_element_type=f32
            )
            dx_ref[:, n : n + part] = dx.astype(bf16)

        def narrow(p, carry):
            to = pl.multiple_of(p * sub, sub)
            for s in range(0, block, 2 * sub):
                halves = []
                for d in (0, sub):
                    row = pl.multiple_of(p * block + s + d, sub)
                    halves.append(
                        jnp.concatenate(
                            [
                                dx_ref[pl.ds(row, sub), j * lanes : (j + 1) * lanes]
                                for j in range(chunks)
                            ],
                            axis=0,
                        )
                    )
                tiles = jnp.dot(
                    swap_ref[...], jnp.concatenate(halves, axis=1), preferred_element_type=f32
                ).astype(bf16)
                for d in (0, 1):
                    e = b * block + s + d * sub
                    back_ref[e : e + sub, pl.ds(to, sub), :] = tiles[
                        :, d * lanes : (d + 1) * lanes
                    ].reshape(sub, sub, lanes)
            return carry

        lax.fori_loop(0, count, narrow, 0, unroll=True)

    for b in range(blocks):
        for i in range(5):
            out_copy(i, b).wait()


def expert_rows(wire, wg, wu, wd, start, count, block, carry=None):
    sources = wire.shape[0]
    width, hidden = wg.shape
    mine = sources * count
    last = carry is not None
    total = sources * capacity
    anywhere = pl.BlockSpec(memory_space=pltpu.HBM)
    high = count * sub + (8 if last else 0)
    back_spec = pl.BlockSpec(
        (pl.Element(sources), pl.Element(high), pl.Element(lanes)),
        lambda i: (0, start * sub, 0),
    )
    out_shape = [
        jax.ShapeDtypeStruct((total, width), bf16),
        jax.ShapeDtypeStruct((total, width), bf16),
        jax.ShapeDtypeStruct((total, hidden), bf16),
        jax.ShapeDtypeStruct((total, hidden), bf16),
        jax.ShapeDtypeStruct((total, hidden), bf16),
        jax.ShapeDtypeStruct((sources, capacity * sub + 8, lanes), bf16),
    ]
    out_specs = [anywhere] * 5 + [back_spec]
    in_specs = [anywhere, pl.BlockSpec(memory_space=pltpu.VMEM), anywhere, anywhere]
    args = [wire, pltpu.with_memory_space_constraint(wg, pltpu.VMEM), wu, wd]
    aliases = {}
    if last:
        in_specs += [anywhere] * 7
        args += [carry[6]] + list(carry[:6])
        aliases = {5 + i: i for i in range(6)}
    else:
        out_specs.append(whole((sources, lanes)))
        out_shape.append(jax.ShapeDtypeStruct((sources, lanes), f32))
    scratch = []
    if last:
        scratch = [pltpu.VMEM((sources, lanes), f32), pltpu.SemaphoreType.DMA]
    return pl.pallas_call(
        functools.partial(expert_kernel, start, count, block, last),
        grid=(1,),
        in_specs=in_specs,
        out_specs=out_specs,
        out_shape=out_shape,
        scratch_shapes=[
            pltpu.VMEM(wire.shape, bf16),
            pltpu.VMEM((width, hidden), bf16),
            pltpu.VMEM((hidden, width), bf16),
            pltpu.VMEM((mine, width), bf16),
            pltpu.VMEM((mine, width), bf16),
            pltpu.VMEM((mine, hidden), bf16),
            pltpu.VMEM((mine, hidden), bf16),
            pltpu.VMEM((mine, hidden), bf16),
            pltpu.VMEM((block * count, width), bf16),
            pltpu.VMEM((sub * sub, sub * sub), bf16),
            pltpu.SemaphoreType.DMA((sources // block, 2, 2)),
            pltpu.SemaphoreType.DMA((2,)),
            pltpu.SemaphoreType.DMA((5, sources // block)),
        ]
        + scratch,
        input_output_aliases=aliases,
        compiler_params=params(60),
        cost_estimate=pl.CostEstimate(
            flops=10 * mine * width * hidden,
            bytes_accessed=6 * width * hidden + 12 * mine * width,
            transcendentals=mine * hidden,
        ),
        name="expert_rows_last" if last else "expert_rows_first",
    )(*args)


def combine_kernel(spot_ref, code_ref, num_ref, back_ref, side_ref, tok_ref, gate_ref, tiles_ref):
    toks, width = tok_ref.shape
    top = code_ref.shape[0]
    chunks = width // lanes
    experts = back_ref.shape[0]
    flat_ref = back_ref.reshape(experts * capacity * sub, lanes)

    def one(t, carry):
        total = None
        for k in range(top):
            at = pl.multiple_of(spot_ref[k, t], sub)
            row = flat_ref[pl.ds(at, sub), :].astype(f32)
            total = row if total is None else total + row
        tiles_ref[t] = total.astype(bf16)
        return carry

    lax.fori_loop(0, toks, one, 0, unroll=8)
    swap = swap_matrix()
    for r in range(0, toks, 2 * sub):
        tiles = jnp.concatenate(
            [tiles_ref[r + d : r + d + sub].reshape(sub * sub, lanes) for d in (0, sub)], axis=1
        )
        flat = jnp.dot(swap, tiles, preferred_element_type=f32).astype(bf16)
        for d in (0, 1):
            for j in range(chunks):
                tok_ref[r + d * sub : r + (d + 1) * sub, j * lanes : (j + 1) * lanes] = flat[
                    j * sub : (j + 1) * sub, d * lanes : (d + 1) * lanes
                ]

    grads = jnp.max(side_ref[...].astype(f32), axis=1)
    grads = jnp.transpose(grads).astype(bf16)
    gate = num_ref[...].astype(f32) * (1.0 / 256.0)
    expert_at = lax.broadcasted_iota(jnp.int32, (experts, toks), 0)
    place_at = lax.broadcasted_iota(jnp.int32, (lanes, toks), 0)
    found = []
    for k in range(top):
        code = code_ref[k : k + 1, :]
        hit = jnp.where((code >> 4) == expert_at, 1.0, 0.0).astype(bf16)
        rows = jnp.dot(grads, hit, preferred_element_type=f32)
        found.append(jnp.sum(jnp.where((code & 15) == place_at, rows, 0.0), axis=0, keepdims=True))
    gate_ref[...] = (jnp.concatenate(found, axis=0) / gate).astype(bf16)


def combine(spot, code, num, back, toks, width):
    top = code.shape[0]
    experts = back.shape[0]

    def rows_of(at, count):
        return pl.BlockSpec(
            (pl.Element(experts), pl.Element(count), pl.Element(lanes)), lambda i: (0, at, 0)
        )

    return pl.pallas_call(
        combine_kernel,
        grid=(1,),
        in_specs=[
            pl.BlockSpec(memory_space=pltpu.SMEM),
            whole(code.shape),
            whole(num.shape),
            rows_of(0, capacity * sub),
            rows_of(capacity * sub, 8),
        ],
        out_specs=[whole((toks, width)), whole((top, toks))],
        out_shape=[
            jax.ShapeDtypeStruct((toks, width), bf16),
            jax.ShapeDtypeStruct((top, toks), bf16),
        ],
        scratch_shapes=[pltpu.VMEM((toks, width // lanes, lanes), bf16)],
        compiler_params=params(60),
        name="combine_rows",
    )(spot, code, num, back, back)


def exchange(rows):
    return lax.all_to_all(rows, ("dp", "expert"), split_axis=0, concat_axis=0, tiled=True)


def local(tokens, d_out, expert_ids, gate_num, w_gate, w_up, w_down):
    toks, width = tokens.shape
    experts = lax.axis_size("dp") * lax.axis_size("expert")
    wg, wu, wd = w_gate[0], w_up[0], w_down[0]
    ids, num = expert_ids.T, gate_num.T
    rest = capacity - first_rows
    first, index, scale, code, spot = pack(tokens, d_out, 0, first_rows, experts, ids, num)
    (second,) = pack(tokens, d_out, first_rows, rest, experts, tables=(index, scale))
    first, second = exchange(first), exchange(second)
    part = expert_rows(first, wg, wu, wd, 0, first_rows, 64)
    rows_x, rows_dy, h, da, db, back = expert_rows(second, wg, wu, wd, first_rows, rest, 128, part)
    back = exchange(back)
    grad_gate = lax.dot_general(rows_x, da, contract_rows, preferred_element_type=f32).astype(bf16)
    grad_up = lax.dot_general(rows_x, db, contract_rows, preferred_element_type=f32).astype(bf16)
    grad_down = lax.dot_general(h, rows_dy, contract_rows, preferred_element_type=f32).astype(bf16)
    d_tokens, d_gate = combine(spot, code, num, back, toks, width)
    return (d_tokens, d_gate.T, grad_gate[None], grad_up[None], grad_down[None])


def solution(mesh):
    rows = P(("dp", "expert"), None)
    blocks = P(("dp", "expert"), None, None)
    return jax.shard_map(
        local,
        mesh=mesh,
        in_specs=(rows, rows, rows, rows, blocks, blocks, blocks),
        out_specs=(rows, rows, blocks, blocks, blocks),
        check_vma=False,
    )
```

```python
import functools

import jax
import jax.numpy as jnp
from jax import lax
from jax.experimental import pallas as pl
from jax.experimental.pallas import tpu as pltpu
from jax.sharding import PartitionSpec as P

bf16 = jnp.bfloat16
f32 = jnp.float32
lanes = 128
sub = 16
capacity = 9
first_rows = 7
contract_rows = (((0,), (0,)), ((), ()))
contract_cols = (((1,), (1,)), ((), ()))


def params(mib):
    return pltpu.CompilerParams(vmem_limit_bytes=mib * 1024 * 1024)


def whole(shape):
    return pl.BlockSpec(shape, lambda *_: (0,) * len(shape))


def swap_matrix():
    size = sub * sub
    row = lax.broadcasted_iota(jnp.int32, (size, size), 0)
    col = lax.broadcasted_iota(jnp.int32, (size, size), 1)
    return jnp.where(((row & 15) << 4) + (row >> 4) == col, 1.0, 0.0).astype(bf16)


def spread_tables(ids, num, experts):
    top, toks = ids.shape
    gate = num.astype(f32) * (1.0 / 256.0)
    expert_at = lax.broadcasted_iota(jnp.int32, (experts, toks), 0)
    named = jnp.zeros((experts, toks), f32)
    gates = jnp.zeros((experts, toks), f32)
    for k in range(top):
        hit = ids[k : k + 1, :] == expert_at
        named = jnp.where(hit, 1.0, named)
        gates = jnp.where(hit, gate[k : k + 1, :], gates)
    row = lax.broadcasted_iota(jnp.int32, (toks, toks), 0)
    col = lax.broadcasted_iota(jnp.int32, (toks, toks), 1)
    before = jnp.where(row < col, 1.0, 0.0).astype(bf16)
    place = jnp.dot(named.astype(bf16), before, preferred_element_type=f32)
    token = lax.broadcasted_iota(jnp.int32, (experts, toks), 1).astype(f32)
    here = [(named > 0.0) & (place == float(p)) for p in range(capacity)]
    wanted = lax.broadcasted_iota(jnp.int32, (sub, capacity * toks), 0)
    owner = lax.broadcasted_iota(jnp.int32, (sub, capacity * toks), 1) >> 7
    collect = jnp.where(owner == wanted, 1.0, 0.0).astype(bf16)
    index, scale = [
        lax.dot_general(
            collect,
            jnp.concatenate([jnp.where(h, v, 0.0).astype(bf16) for h in here], axis=1),
            contract_cols,
            preferred_element_type=f32,
        )
        for v in (token, gates)
    ]
    code = (expert_at * sub).astype(f32) + place
    spot = (expert_at * (capacity * sub)).astype(f32) + place * float(sub)
    codes, spots = [
        jnp.concatenate(
            [
                jnp.sum(jnp.where(ids[k : k + 1, :] == expert_at, v, 0.0), axis=0, keepdims=True)
                for k in range(top)
            ],
            axis=0,
        ).astype(jnp.int32)
        for v in (code, spot)
    ]
    return index.astype(jnp.int32), scale, codes, spots


def wide_to_tiles(swap, wide, chunks, store):
    rows = wide.shape[0]
    for r in range(0, rows, 2 * sub):
        halves = [
            jnp.concatenate(
                [wide[r + d : r + d + sub, j * lanes : (j + 1) * lanes] for j in range(chunks)], axis=0
            )
            for d in (0, sub)
        ]
        tiles = jnp.dot(swap, jnp.concatenate(halves, axis=1), preferred_element_type=f32)
        store(r, tiles[:, :lanes].reshape(sub, chunks, lanes))
        store(r + sub, tiles[:, lanes:].reshape(sub, chunks, lanes))


def make_tiles(tok_ref, dy_ref, tok_tiles, dy_tiles):
    swap = swap_matrix()
    chunks = tok_ref.shape[1] // lanes

    def put_tok(r, tiles):
        tok_tiles[r : r + sub] = tiles.astype(bf16)

    def put_dy(r, tiles):
        dy_tiles[r : r + sub] = tiles

    wide_to_tiles(swap, tok_ref, chunks, put_tok)
    wide_to_tiles(swap, dy_ref, chunks, put_dy)


def fill_rows(start, count, index_ref, scale_ref, tok_tiles, dy_tiles, buffer, out_hbm, sems):
    experts = buffer.shape[0]
    groups = sems.shape[0]
    group = experts // groups

    def out_copy(g):
        at = slice(g * group, (g + 1) * group)
        return pltpu.make_async_copy(buffer.at[at], out_hbm.at[at], sems.at[g])

    def one(e, carry):
        for p in range(count):
            token = index_ref[start + p, e]
            scale = scale_ref[start + p, e]
            buffer[e, p * sub : (p + 1) * sub, :] = tok_tiles[token]
            at = (count + p) * sub
            buffer[e, at : at + sub, :] = (dy_tiles[token] * scale).astype(bf16)
        return carry

    for g in range(groups):
        lax.fori_loop(g * group, (g + 1) * group, one, 0, unroll=2)
        out_copy(g).start()
    for g in range(groups):
        out_copy(g).wait()


def pack_first_kernel(
    start, count, ids_ref, num_ref, tok_hbm, dy_hbm,
    out_hbm, index_ref, scale_ref, code_ref, spot_ref,
    tok_tiles, dy_tiles, buffer, out_sems, index_s, scale_s, tok_ref, dy_ref, sems,
):
    tok_in = pltpu.make_async_copy(tok_hbm, tok_ref, sems.at[2])
    dy_in = pltpu.make_async_copy(dy_hbm, dy_ref, sems.at[3])
    tok_in.start()
    dy_in.start()
    index, scale, code, spot = spread_tables(ids_ref[...], num_ref[...], index_ref.shape[1])
    index_ref[...] = index
    scale_ref[...] = scale
    one = pltpu.make_async_copy(index_ref, index_s, sems.at[0])
    two = pltpu.make_async_copy(scale_ref, scale_s, sems.at[1])
    one.start()
    two.start()
    code_ref[...] = code
    spot_ref[...] = spot
    tok_in.wait()
    dy_in.wait()
    make_tiles(tok_ref, dy_ref, tok_tiles, dy_tiles)
    one.wait()
    two.wait()
    fill_rows(start, count, index_s, scale_s, tok_tiles, dy_tiles, buffer, out_hbm, out_sems)


def pack_rest_kernel(
    start, count, index_ref, scale_ref, tok_ref, dy_ref,
    out_hbm, tok_tiles, dy_tiles, buffer, out_sems,
):
    make_tiles(tok_ref, dy_ref, tok_tiles, dy_tiles)
    fill_rows(start, count, index_ref, scale_ref, tok_tiles, dy_tiles, buffer, out_hbm, out_sems)


def pack(tokens, d_out, start, count, experts, ids=None, num=None, tables=None):
    toks, width = tokens.shape
    chunks = width // lanes
    wire = (experts, 2 * count * sub, lanes)
    out_shape = [jax.ShapeDtypeStruct(wire, bf16)]
    out_specs = [pl.BlockSpec(memory_space=pl.ANY)]
    scratch = [
        pltpu.VMEM((toks, chunks, lanes), bf16),
        pltpu.VMEM((toks, chunks, lanes), f32),
        pltpu.VMEM(wire, bf16),
        pltpu.SemaphoreType.DMA((16,)),
    ]
    vmem = pl.BlockSpec(memory_space=pltpu.VMEM)
    if tables is None:
        body = functools.partial(pack_first_kernel, start, count)
        args = (ids, num, tokens, d_out)
        in_specs = [vmem] * 2 + [pl.BlockSpec(memory_space=pl.ANY)] * 2
        out_shape += [
            jax.ShapeDtypeStruct((sub, experts), jnp.int32),
            jax.ShapeDtypeStruct((sub, experts), f32),
            jax.ShapeDtypeStruct(ids.shape, jnp.int32),
            jax.ShapeDtypeStruct(ids.shape, jnp.int32),
        ]
        out_specs += [vmem] * 4
        scratch += [
            pltpu.SMEM((sub, experts), jnp.int32),
            pltpu.SMEM((sub, experts), f32),
            pltpu.VMEM(tokens.shape, bf16),
            pltpu.VMEM(d_out.shape, bf16),
            pltpu.SemaphoreType.DMA((4,)),
        ]
    else:
        body = functools.partial(pack_rest_kernel, start, count)
        args = (*tables, tokens, d_out)
        in_specs = [pl.BlockSpec(memory_space=pltpu.SMEM)] * 2 + [vmem] * 2
    return pl.pallas_call(
        body,
        in_specs=in_specs,
        out_specs=out_specs,
        out_shape=out_shape,
        scratch_shapes=scratch,
        compiler_params=params(60),
        cost_estimate=pl.CostEstimate(
            flops=0, bytes_accessed=4 * experts * count * width, transcendentals=0
        ),
        name="pack_first" if tables is None else "pack_rest",
    )(*args)


def expert_kernel(start, count, block, last, *refs):
    (wire_hbm, wg, wu_hbm, wd_hbm) = refs[:4]
    refs = refs[4:]
    if last:
        old_gate_hbm = refs[0]
        refs = refs[7:]
    out_hbm = refs[:5]
    back_ref = refs[5]
    refs = refs[6:]
    if not last:
        gate_ref = refs[0]
        refs = refs[1:]
    (wire, wu, wd, x_ref, dy_ref, h_ref, da_ref, db_ref, dx_ref, swap_ref) = refs[:10]
    (wire_sem, weight_sem, out_sem) = refs[10:13]
    if last:
        (old_gate_ref, old_gate_sem) = refs[13:]
        old_gate = pltpu.make_async_copy(old_gate_hbm, old_gate_ref, old_gate_sem)
    sources = wire_hbm.shape[0]
    blocks = sources // block
    rows = block * count
    width, hidden = wg.shape
    chunks = width // lanes
    part = 256
    half = count * sub

    near = 2 * sub
    pieces = range(block // near)

    def wire_copy(b, side, piece):
        low = b * block + piece * near
        at = (slice(low, low + near), slice(side * half, (side + 1) * half))
        return pltpu.make_async_copy(wire_hbm.at[at], wire.at[at], wire_sem.at[b, side, piece])

    def wire_start(b, side):
        for piece in pieces:
            wire_copy(b, side, piece).start()

    weights = [
        pltpu.make_async_copy(src, dst, weight_sem.at[i])
        for i, (src, dst) in enumerate(((wu_hbm, wu), (wd_hbm, wd)))
    ]

    def out_copy(i, b):
        src = (x_ref, dy_ref, h_ref, da_ref, db_ref)[i]
        to = sources * start + b * rows
        return pltpu.make_async_copy(
            src.at[b * rows : (b + 1) * rows], out_hbm[i].at[to : to + rows], out_sem.at[i, b]
        )

    wire_start(0, 0)
    weights[0].start()
    wire_start(0, 1)
    weights[1].start()
    for b in range(1, blocks):
        wire_start(b, 0)
        wire_start(b, 1)
    if last:
        old_gate.start()
    swap_ref[...] = swap_matrix()

    def widen(b, side, piece, out):
        def step(p, carry):
            at = pl.multiple_of(side * half + p * sub, sub)
            for s in range(piece * near, (piece + 1) * near, 2 * sub):
                tiles = jnp.concatenate(
                    [
                        wire[b * block + s + d : b * block + s + d + sub, pl.ds(at, sub), :].reshape(
                            sub * sub, lanes
                        )
                        for d in (0, sub)
                    ],
                    axis=1,
                )
                flat = jnp.dot(swap_ref[...], tiles, preferred_element_type=f32).astype(bf16)
                for d in (0, 1):
                    to = pl.multiple_of(b * rows + p * block + s + d * sub, sub)
                    for j in range(chunks):
                        out[pl.ds(to, sub), j * lanes : (j + 1) * lanes] = flat[
                            j * sub : (j + 1) * sub, d * lanes : (d + 1) * lanes
                        ]
            return carry

        lax.fori_loop(0, count, step, 0, unroll=True)

    for b in range(blocks):
        low, high = b * rows, (b + 1) * rows
        for piece in pieces:
            wire_copy(b, 0, piece).wait()
            widen(b, 0, piece, x_ref)
        out_copy(0, b).start()
        gates_in = [
            jnp.dot(x_ref[low:high], wg[:, n : n + part], preferred_element_type=f32)
            for n in range(0, hidden, part)
        ]
        for piece in pieces:
            wire_copy(b, 1, piece).wait()
            widen(b, 1, piece, dy_ref)
        out_copy(1, b).start()
        if b == 0:
            for copy in weights:
                copy.wait()

        gate_grad = jnp.zeros((rows, 1), f32)
        for n in range(0, hidden, part):
            x = x_ref[low:high]
            a = gates_in[n // part]
            up = jnp.dot(x, wu[:, n : n + part], preferred_element_type=f32)
            u = lax.dot_general(
                dy_ref[low:high], wd[n : n + part, :], contract_cols, preferred_element_type=f32
            )
            sig = jax.nn.sigmoid(a)
            active = a * sig
            h = active * up
            gate_grad = gate_grad + jnp.sum(u * h, axis=1, keepdims=True)
            h_ref[low:high, n : n + part] = h.astype(bf16)
            da_ref[low:high, n : n + part] = (u * up * sig * (1.0 + a * (1.0 - sig))).astype(bf16)
            db_ref[low:high, n : n + part] = (u * active).astype(bf16)
        for i in (2, 3, 4):
            out_copy(i, b).start()

        lane = lax.broadcasted_iota(jnp.int32, (block, lanes), 1)
        at = slice(b * block, (b + 1) * block)
        if last:
            old_gate.wait()
        gates = old_gate_ref[at, :] if last else jnp.zeros((block, lanes), f32)
        for p in range(count):
            gates = jnp.where(lane == start + p, gate_grad[p * block : (p + 1) * block], gates)
        if last:
            eight = jnp.broadcast_to(gates[:, None, :], (block, 8, lanes))
            back_ref[at, half : half + 8, :] = eight.astype(bf16)
        else:
            gate_ref[at, :] = gates

        for n in range(0, width, part):
            dx = lax.dot_general(
                da_ref[low:high], wg[n : n + part, :], contract_cols, preferred_element_type=f32
            )
            dx = dx + lax.dot_general(
                db_ref[low:high], wu[n : n + part, :], contract_cols, preferred_element_type=f32
            )
            dx_ref[:, n : n + part] = dx.astype(bf16)

        def narrow(p, carry):
            to = pl.multiple_of(p * sub, sub)
            for s in range(0, block, 2 * sub):
                halves = []
                for d in (0, sub):
                    row = pl.multiple_of(p * block + s + d, sub)
                    halves.append(
                        jnp.concatenate(
                            [
                                dx_ref[pl.ds(row, sub), j * lanes : (j + 1) * lanes]
                                for j in range(chunks)
                            ],
                            axis=0,
                        )
                    )
                tiles = jnp.dot(
                    swap_ref[...], jnp.concatenate(halves, axis=1), preferred_element_type=f32
                ).astype(bf16)
                for d in (0, 1):
                    e = b * block + s + d * sub
                    back_ref[e : e + sub, pl.ds(to, sub), :] = tiles[
                        :, d * lanes : (d + 1) * lanes
                    ].reshape(sub, sub, lanes)
            return carry

        lax.fori_loop(0, count, narrow, 0, unroll=True)

    for b in range(blocks):
        for i in range(5):
            out_copy(i, b).wait()


def expert_rows(wire, wg, wu, wd, start, count, block, carry=None):
    sources = wire.shape[0]
    width, hidden = wg.shape
    mine = sources * count
    last = carry is not None
    total = sources * capacity
    anywhere = pl.BlockSpec(memory_space=pltpu.HBM)
    high = count * sub + (8 if last else 0)
    back_spec = pl.BlockSpec(
        (pl.Element(sources), pl.Element(high), pl.Element(lanes)),
        lambda i: (0, start * sub, 0),
    )
    out_shape = [
        jax.ShapeDtypeStruct((total, width), bf16),
        jax.ShapeDtypeStruct((total, width), bf16),
        jax.ShapeDtypeStruct((total, hidden), bf16),
        jax.ShapeDtypeStruct((total, hidden), bf16),
        jax.ShapeDtypeStruct((total, hidden), bf16),
        jax.ShapeDtypeStruct((sources, capacity * sub + 8, lanes), bf16),
    ]
    out_specs = [anywhere] * 5 + [back_spec]
    in_specs = [anywhere, pl.BlockSpec(memory_space=pltpu.VMEM), anywhere, anywhere]
    args = [wire, pltpu.with_memory_space_constraint(wg, pltpu.VMEM), wu, wd]
    aliases = {}
    if last:
        in_specs += [anywhere] * 7
        args += [carry[6]] + list(carry[:6])
        aliases = {5 + i: i for i in range(6)}
    else:
        out_specs.append(whole((sources, lanes)))
        out_shape.append(jax.ShapeDtypeStruct((sources, lanes), f32))
    scratch = []
    if last:
        scratch = [pltpu.VMEM((sources, lanes), f32), pltpu.SemaphoreType.DMA]
    return pl.pallas_call(
        functools.partial(expert_kernel, start, count, block, last),
        grid=(1,),
        in_specs=in_specs,
        out_specs=out_specs,
        out_shape=out_shape,
        scratch_shapes=[
            pltpu.VMEM(wire.shape, bf16),
            pltpu.VMEM((width, hidden), bf16),
            pltpu.VMEM((hidden, width), bf16),
            pltpu.VMEM((mine, width), bf16),
            pltpu.VMEM((mine, width), bf16),
            pltpu.VMEM((mine, hidden), bf16),
            pltpu.VMEM((mine, hidden), bf16),
            pltpu.VMEM((mine, hidden), bf16),
            pltpu.VMEM((block * count, width), bf16),
            pltpu.VMEM((sub * sub, sub * sub), bf16),
            pltpu.SemaphoreType.DMA((sources // block, 2, block // (2 * sub))),
            pltpu.SemaphoreType.DMA((2,)),
            pltpu.SemaphoreType.DMA((5, sources // block)),
        ]
        + scratch,
        input_output_aliases=aliases,
        compiler_params=params(60),
        cost_estimate=pl.CostEstimate(
            flops=10 * mine * width * hidden,
            bytes_accessed=6 * width * hidden + 12 * mine * width,
            transcendentals=mine * hidden,
        ),
        name="expert_rows_last" if last else "expert_rows_first",
    )(*args)


def combine_kernel(spot_ref, code_ref, num_ref, back_ref, side_ref, tok_ref, gate_ref, tiles_ref):
    toks, width = tok_ref.shape
    top = code_ref.shape[0]
    chunks = width // lanes
    experts = back_ref.shape[0]
    flat_ref = back_ref.reshape(experts * capacity * sub, lanes)

    def one(t, carry):
        total = None
        for k in range(top):
            at = pl.multiple_of(spot_ref[k, t], sub)
            row = flat_ref[pl.ds(at, sub), :].astype(f32)
            total = row if total is None else total + row
        tiles_ref[t] = total.astype(bf16)
        return carry

    lax.fori_loop(0, toks, one, 0, unroll=8)
    swap = swap_matrix()
    for r in range(0, toks, 2 * sub):
        tiles = jnp.concatenate(
            [tiles_ref[r + d : r + d + sub].reshape(sub * sub, lanes) for d in (0, sub)], axis=1
        )
        flat = jnp.dot(swap, tiles, preferred_element_type=f32).astype(bf16)
        for d in (0, 1):
            for j in range(chunks):
                tok_ref[r + d * sub : r + (d + 1) * sub, j * lanes : (j + 1) * lanes] = flat[
                    j * sub : (j + 1) * sub, d * lanes : (d + 1) * lanes
                ]

    grads = jnp.max(side_ref[...].astype(f32), axis=1)
    grads = jnp.transpose(grads).astype(bf16)
    gate = num_ref[...].astype(f32) * (1.0 / 256.0)
    expert_at = lax.broadcasted_iota(jnp.int32, (experts, toks), 0)
    place_at = lax.broadcasted_iota(jnp.int32, (lanes, toks), 0)
    found = []
    for k in range(top):
        code = code_ref[k : k + 1, :]
        hit = jnp.where((code >> 4) == expert_at, 1.0, 0.0).astype(bf16)
        rows = jnp.dot(grads, hit, preferred_element_type=f32)
        found.append(jnp.sum(jnp.where((code & 15) == place_at, rows, 0.0), axis=0, keepdims=True))
    gate_ref[...] = (jnp.concatenate(found, axis=0) / gate).astype(bf16)


def combine(spot, code, num, back, toks, width):
    top = code.shape[0]
    experts = back.shape[0]

    def rows_of(at, count):
        return pl.BlockSpec(
            (pl.Element(experts), pl.Element(count), pl.Element(lanes)), lambda i: (0, at, 0)
        )

    return pl.pallas_call(
        combine_kernel,
        grid=(1,),
        in_specs=[
            pl.BlockSpec(memory_space=pltpu.SMEM),
            whole(code.shape),
            whole(num.shape),
            rows_of(0, capacity * sub),
            rows_of(capacity * sub, 8),
        ],
        out_specs=[whole((toks, width)), whole((top, toks))],
        out_shape=[
            jax.ShapeDtypeStruct((toks, width), bf16),
            jax.ShapeDtypeStruct((top, toks), bf16),
        ],
        scratch_shapes=[pltpu.VMEM((toks, width // lanes, lanes), bf16)],
        compiler_params=params(60),
        name="combine_rows",
    )(spot, code, num, back, back)


def exchange(rows):
    return lax.all_to_all(rows, ("dp", "expert"), split_axis=0, concat_axis=0, tiled=True)


def local(tokens, d_out, expert_ids, gate_num, w_gate, w_up, w_down):
    toks, width = tokens.shape
    experts = lax.axis_size("dp") * lax.axis_size("expert")
    wg, wu, wd = w_gate[0], w_up[0], w_down[0]
    ids, num = expert_ids.T, gate_num.T
    rest = capacity - first_rows
    first, index, scale, code, spot = pack(tokens, d_out, 0, first_rows, experts, ids, num)
    (second,) = pack(tokens, d_out, first_rows, rest, experts, tables=(index, scale))
    first, second = exchange(first), exchange(second)
    part = expert_rows(first, wg, wu, wd, 0, first_rows, 64)
    rows_x, rows_dy, h, da, db, back = expert_rows(second, wg, wu, wd, first_rows, rest, 128, part)
    back = exchange(back)
    grad_gate = lax.dot_general(rows_x, da, contract_rows, preferred_element_type=f32).astype(bf16)
    grad_up = lax.dot_general(rows_x, db, contract_rows, preferred_element_type=f32).astype(bf16)
    grad_down = lax.dot_general(h, rows_dy, contract_rows, preferred_element_type=f32).astype(bf16)
    d_tokens, d_gate = combine(spot, code, num, back, toks, width)
    return (d_tokens, d_gate.T, grad_gate[None], grad_up[None], grad_down[None])


def solution(mesh):
    rows = P(("dp", "expert"), None)
    blocks = P(("dp", "expert"), None, None)
    return jax.shard_map(
        local,
        mesh=mesh,
        in_specs=(rows, rows, rows, rows, blocks, blocks, blocks),
        out_specs=(rows, rows, blocks, blocks, blocks),
        check_vma=False,
    )
```
